512 devices in a mesh: rcv: 128 (over y, x, z_lo), frq: 4 (over z_hi, core).
Axes of the slice: x: 4, y: 4, z: 16 (z_hi: 2, z_lo: 8; z = z_hi * 8 + z_lo), core: 2. Of those that a mesh axis runs over, the one named last changes fastest.
Arguments:
- traces: bfloat16 [32, 2048, 2048], P(None, 'rcv', 'frq'), may hold values from -6 to 6
- taper_start: int32 [2048], P('rcv'), may hold values from 0 to 1023
- taper_stop: int32 [2048], P('rcv'), may hold values from 1024 to 2048
- freq_index: int32 [16], replicated, may hold values from 1472 to 1535, as said below
- kernel: bfloat16 [2, 16, 2048, 2048], P(None, 'frq', 'rcv'), may hold values from -0.5 to 0.5
Outputs:
- output_traces: float32 [32, 2048, 2048], P(None, 'rcv', 'frq')
The draws below stay inside these ranges and needn't reach their ends.
Inputs may be any that keep to these rules, and one draw needn't show every extreme that they name: `freq_index`: distinct and increasing; the first is always the smallest allowed bin and the last always the largest.
All inputs are finite; a program needn't handle non-finite values.
Results may differ from the reference program's by a relative error of at most 0.0052.
Values may be sent and summed in bfloat16 or wider, within the bound.
A program may use at most 64 MiB of HBM per device.

```python
import math
import jax
import jax.numpy as jnp
from jax import lax

VIRTUAL_ROWS = 32
RECEIVER_COUNT = 2048
SOURCE_COUNT = 2048
BAND_FREQUENCIES = 16
TRACE_SAMPLES = 2048
PADDED_LENGTH = 3072


def draw_freq_index(key, part):
    key = jax.random.fold_in(key, 7)
    base = PADDED_LENGTH // 2 - 4 * BAND_FREQUENCIES
    picks = jax.random.permutation(key, 4 * BAND_FREQUENCIES - 2)[:BAND_FREQUENCIES - 2] + 1
    inner = jnp.sort(picks)
    offsets = jnp.concatenate([jnp.zeros((1,), jnp.int32), inner.astype(jnp.int32), jnp.full((1,), 4 * BAND_FREQUENCIES - 1, jnp.int32)])
    return (base + offsets).astype(jnp.int32)


def with_ends(array, key, low, top_value):
    longest = array.shape.index(max(array.shape))
    spots = []
    for shift in (0, 1):
        where = [jax.random.randint(jax.random.fold_in(key, axis), (), 0, length) for axis, length in enumerate(array.shape)]
        where[longest] = (where[longest] + shift) % array.shape[longest]
        spots.append(tuple(where))
    return array.at[spots[0]].set(low).at[spots[1]].set(top_value)


def with_spikes(drawn, rng, source, target, shards_of, factor):
    def block_of(position):
        return (jnp.arange(drawn.shape[position]) // (drawn.shape[position] // shards_of)).reshape((-1,) + (1,) * (drawn.ndim - 1 - position))

    first = jax.random.permutation(rng, shards_of)[block_of(target)]
    second = (block_of(target) + shards_of // 2) % shards_of
    return jnp.where((block_of(source) == first) | (block_of(source) == second), factor * drawn, drawn)


def block_levels(key, dims, cuts, least, top_value):
    gain = 1.0
    for position, shards_of in cuts:
        heights = jax.random.uniform(jax.random.fold_in(jax.random.fold_in(key, 6), position), (shards_of,), jnp.float32, least / len(cuts), top_value / len(cuts))
        gain = gain * jnp.repeat(jnp.exp(heights), dims[position] // shards_of).reshape((-1,) + (1,) * (len(dims) - 1 - position))
    return gain


def bell_draw(stream_key, extent, width, limit, cuts=(), kind=jnp.bfloat16):
    array = width * jax.random.normal(stream_key, extent, jnp.float32)
    if cuts:
        array = array * block_levels(stream_key, extent, cuts, -0.22, 0.18)
    return jnp.clip(array, -limit, limit).astype(kind)


def heavy_noise(own_key, shape, spread, limit, split, heavy, held_as=jnp.bfloat16):
    entries = spread * jax.random.normal(own_key, shape, jnp.float32)
    if split:
        entries = entries * block_levels(own_key, shape, split, -0.22, 0.18)
    return jnp.clip(with_spikes(entries, jax.random.fold_in(own_key, 3), *heavy), -limit, limit).astype(held_as)


def setup_inputs(seed: int = 0) -> dict:
    splits = jax.random.split(jax.random.key(seed), 6)
    return {
        "traces": bell_draw(splits[0], (VIRTUAL_ROWS, RECEIVER_COUNT, TRACE_SAMPLES), 1.0, 6.0, ((1, 128), (2, 4))),
        "taper_start": with_ends(jax.random.randint(splits[1], (RECEIVER_COUNT,), 0, TRACE_SAMPLES // 2), jax.random.fold_in(splits[1], 1), 0, (TRACE_SAMPLES // 2) - 1).astype(jnp.int32),
        "taper_stop": with_ends(jax.random.randint(splits[2], (RECEIVER_COUNT,), TRACE_SAMPLES // 2, TRACE_SAMPLES + 1), jax.random.fold_in(splits[2], 1), TRACE_SAMPLES // 2, TRACE_SAMPLES).astype(jnp.int32),
        "freq_index": draw_freq_index(jax.random.fold_in(splits[5], 71), 0),
        "kernel": heavy_noise(splits[4], (2, BAND_FREQUENCIES, RECEIVER_COUNT, SOURCE_COUNT), RECEIVER_COUNT ** -0.5, 0.5, ((1, 4), (2, 128)), (2, 3, 128, 5.5)),
    }


def phase_tables(freq_bins, sample_times):
    product = freq_bins[:, None] * sample_times[None, :] % PADDED_LENGTH
    phase = product.astype(jnp.float32) * (2.0 * math.pi / PADDED_LENGTH)
    return (jnp.cos(phase).astype(jnp.bfloat16), (-jnp.sin(phase)).astype(jnp.bfloat16))

def reference(traces, taper_start, taper_stop, freq_index, kernel):
    sample_times = jnp.arange(TRACE_SAMPLES, dtype=jnp.int32)
    window = (sample_times[None, :] >= taper_start[:, None]) & (sample_times[None, :] < taper_stop[:, None])
    tapered_traces = traces * window.astype(jnp.bfloat16)[None, :, :]
    cosine, sine = phase_tables(freq_index, sample_times)
    forward_spectra = jnp.concatenate([cosine, sine], axis=0).T
    trace_spectra = jnp.dot(tapered_traces.reshape(VIRTUAL_ROWS * RECEIVER_COUNT, TRACE_SAMPLES), forward_spectra, preferred_element_type=jnp.float32)
    trace_spectra = (trace_spectra * (1.0 / math.sqrt(PADDED_LENGTH))).reshape(VIRTUAL_ROWS, RECEIVER_COUNT, 2, BAND_FREQUENCIES)
    trace_spectra = trace_spectra.transpose(3, 2, 0, 1).astype(jnp.bfloat16)

    def one_freq(index):
        real_part = trace_spectra[index, 0]
        imag_part = trace_spectra[index, 1]
        stacked = jnp.concatenate([jnp.concatenate([real_part, imag_part], axis=1), jnp.concatenate([imag_part, -real_part], axis=1)], axis=0)
        kernel_rows = jnp.concatenate([kernel[0, index], kernel[1, index]], axis=0)
        return jnp.dot(stacked, kernel_rows, preferred_element_type=jnp.float32).astype(jnp.bfloat16)
    kernel_response = lax.map(one_freq, jnp.arange(BAND_FREQUENCIES, dtype=jnp.int32))
    kernel_response = kernel_response.reshape(BAND_FREQUENCIES, 2, VIRTUAL_ROWS, SOURCE_COUNT)
    inverse = jnp.concatenate([cosine, sine], axis=0)
    arranged_rows = kernel_response.transpose(2, 3, 1, 0).reshape(VIRTUAL_ROWS * SOURCE_COUNT, 2 * BAND_FREQUENCIES)
    adjoint_output = jnp.dot(arranged_rows, inverse, preferred_element_type=jnp.float32) * (1.0 / math.sqrt(BAND_FREQUENCIES))
    return adjoint_output.reshape(VIRTUAL_ROWS, SOURCE_COUNT, TRACE_SAMPLES)
```

```python
import math

import jax
import jax.numpy as jnp
from jax import lax
from jax.experimental import pallas as pl
from jax.experimental.pallas import tpu as pltpu
from jax.sharding import PartitionSpec as P

BAND_FREQUENCIES = 16
PADDED_LENGTH = 3072
MESH = pl.DeviceIdType.MESH

ROWS = 32
RCV = 16
TIME = 512
FREQS = 4
PLANE = 16
LINE = 8
GROUPS = 4
FC = 2 * FREQS
LANES = FC * ROWS
SRC = 128


def iota(shape, axis):
    return lax.broadcasted_iota(jnp.int32, shape, axis)


def column(ref, count, shape):
    rows = shape[0]
    each = rows // count
    row = iota(shape, 0) // each
    out = jnp.full(shape, ref[0], jnp.int32)
    for i in range(1, count):
        out = jnp.where(row == i, ref[i], out)
    return out


def tables(freq_ref, first_sample):
    shape = (2 * BAND_FREQUENCIES, TIME)
    bins = column(freq_ref, BAND_FREQUENCIES, shape)
    steps = bins * (first_sample + iota(shape, 1)) + (iota(shape, 0) % 2) * (PADDED_LENGTH // 4)
    steps = steps.astype(jnp.float32)
    steps = steps - jnp.floor(steps * (1.0 / PADDED_LENGTH)) * PADDED_LENGTH
    steps = jnp.where(steps < 0, steps + PADDED_LENGTH, steps)
    steps = jnp.where(steps >= PADDED_LENGTH, steps - PADDED_LENGTH, steps)
    x = (jnp.abs(steps - PADDED_LENGTH // 2) - PADDED_LENGTH // 4) * (2.0 * math.pi / PADDED_LENGTH)
    y = x * x
    poly = jnp.full(shape, -1.0 / math.factorial(11), jnp.float32)
    for power in (9, 7, 5, 3, 1):
        sign = 1.0 if power % 4 == 1 else -1.0
        poly = poly * y + sign / math.factorial(power)
    return x * poly


def body(
    start_ref,
    stop_ref,
    freq_ref,
    traces_ref,
    kernel_ref,
    out_ref,
    tr_buf,
    kbuf,
    pbuf,
    fbuf,
    gbuf,
    part,
    zbuf,
    rbuf,
    texp,
    lhs,
    local_sem,
    ks_sem,
    kr_sem,
    fs_sem,
    fr_sem,
    gs_sem,
    gr_sem,
    zs_sem,
    zr_sem,
    rs_sem,
    rr_sem,
):
    rcv = lax.axis_index("rcv")
    frq = lax.axis_index("frq")
    plane = rcv // LINE
    line = rcv % LINE

    def on_plane(i):
        peer = (plane + i) % PLANE
        return peer, (peer * LINE + line, frq)

    def on_line(i):
        peer = (line + i) % LINE
        return peer, (plane * LINE + peer, frq)

    def on_frq(i):
        peer = (frq + i) % GROUPS
        return peer, (rcv, peer)

    barrier = pltpu.get_barrier_semaphore()
    for near, count in ((on_plane, PLANE), (on_line, LINE), (on_frq, GROUPS)):

        @pl.loop(1, count)
        def _(i, near=near):
            pl.semaphore_signal(barrier, inc=1, device_id=near(i)[1], device_id_type=MESH)

    traces_copy = pltpu.make_async_copy(traces_ref, tr_buf, local_sem.at[0])
    traces_copy.start()

    def columns(peer):
        return kernel_ref.at[:, :, :, pl.ds(pl.multiple_of(peer * SRC, SRC), SRC)]

    own_copy = pltpu.make_async_copy(columns(plane), kbuf.at[:, :, plane], local_sem.at[1])
    own_copy.start()

    table = tables(freq_ref, frq * TIME).astype(jnp.bfloat16)

    pl.semaphore_wait(barrier, PLANE + LINE + GROUPS - 3)

    def kernel_send(i):
        peer, device = on_plane(i)
        return pltpu.make_async_remote_copy(
            src_ref=columns(peer),
            dst_ref=kbuf.at[:, :, plane],
            send_sem=ks_sem.at[peer],
            recv_sem=kr_sem.at[plane],
            device_id=device,
            device_id_type=MESH,
        )

    def kernel_recv(i):
        peer, device = on_plane(i)
        return pltpu.make_async_remote_copy(
            src_ref=columns(peer),
            dst_ref=kbuf.at[:, :, peer],
            send_sem=ks_sem.at[peer],
            recv_sem=kr_sem.at[peer],
            device_id=device,
            device_id_type=MESH,
        )

    @pl.loop(1, PLANE)
    def _(i):
        kernel_send(i).start()

    sample = frq * TIME + iota((RCV, TIME), 1)
    start = column(start_ref, RCV, (RCV, TIME))
    stop = column(stop_ref, RCV, (RCV, TIME))
    window = jnp.where((sample >= start) & (sample < stop), 1.0, 0.0).astype(jnp.bfloat16)
    traces_copy.wait()
    tapered = (tr_buf[...] * window[None]).reshape(ROWS * RCV, TIME)
    pbuf[...] = lax.dot_general(
        table, tapered, (((1,), (1,)), ((), ())), preferred_element_type=jnp.float32
    )

    def rows_of(peer):
        return pl.ds(pl.multiple_of(peer * FC, FC), FC)

    def sums_copy(i, to):
        peer, device = on_frq(i)
        slot = frq if to else peer
        return pltpu.make_async_remote_copy(
            src_ref=pbuf.at[rows_of(peer)],
            dst_ref=fbuf.at[slot],
            send_sem=fs_sem.at[peer],
            recv_sem=fr_sem.at[slot],
            device_id=device,
            device_id_type=MESH,
        )

    for i in range(1, GROUPS):
        sums_copy(i, True).start()
    fbuf[frq] = pbuf[rows_of(frq)]

    for i in range(2 * BAND_FREQUENCIES):
        texp[i * ROWS : (i + 1) * ROWS] = jnp.broadcast_to(table[i : i + 1], (ROWS, TIME))

    for i in range(1, GROUPS):
        sums_copy(i, False).wait_recv()
    total = ((fbuf[0] + fbuf[1]) + (fbuf[2] + fbuf[3])) * (1.0 / math.sqrt(PADDED_LENGTH))
    wide = jnp.broadcast_to(total[:, None, :], (FC, ROWS, ROWS * RCV))
    own_row = iota((FC, ROWS, ROWS * RCV), 2) // RCV == iota((FC, ROWS, ROWS * RCV), 1)
    wide = jnp.where(own_row, wide, 0.0).astype(jnp.bfloat16).reshape(LANES, ROWS * RCV)
    pick = (iota((RCV, ROWS * RCV), 1) % RCV == iota((RCV, ROWS * RCV), 0)).astype(jnp.float32)
    spectra = lax.dot_general(
        pick.astype(jnp.bfloat16), wide, (((1,), (1,)), ((), ())), preferred_element_type=jnp.float32
    )
    gbuf[plane] = spectra.astype(jnp.bfloat16)

    def spectra_copy(i, to):
        peer, device = on_plane(i)
        slot = plane if to else peer
        return pltpu.make_async_remote_copy(
            src_ref=gbuf.at[plane],
            dst_ref=gbuf.at[slot],
            send_sem=gs_sem.at[peer],
            recv_sem=gr_sem.at[slot],
            device_id=device,
            device_id_type=MESH,
        )

    @pl.loop(1, PLANE)
    def _(i):
        spectra_copy(i, True).start()

    own_copy.wait()

    @pl.loop(1, PLANE)
    def _(i):
        kernel_recv(i).wait_recv()

    @pl.loop(1, PLANE)
    def _(i):
        spectra_copy(i, False).wait_recv()

    for pair in range(FREQS // 2):
        flipped = gbuf[:, :, pair * 128 : (pair + 1) * 128].reshape(PLANE * RCV, 128)
        flipped = flipped.astype(jnp.float32).T
        halves = []
        for f in range(2):
            real = flipped[f * 64 : f * 64 + 32]
            imag = flipped[f * 64 + 32 : f * 64 + 64]
            left = jnp.concatenate([real, imag], axis=0).astype(jnp.bfloat16)
            right = jnp.concatenate([imag, -real], axis=0).astype(jnp.bfloat16)
            halves.append(
                jnp.dot(
                    left,
                    kbuf[0, pair * 2 + f].reshape(PLANE * RCV, SRC),
                    preferred_element_type=jnp.float32,
                )
                + jnp.dot(
                    right,
                    kbuf[1, pair * 2 + f].reshape(PLANE * RCV, SRC),
                    preferred_element_type=jnp.float32,
                )
            )
        part[:, pair * 128 : (pair + 1) * 128] = jnp.concatenate(halves, axis=0).T

    def source_rows(peer):
        return pl.ds(pl.multiple_of(peer * RCV, RCV), RCV)

    def line_copy(i, to):
        peer, device = on_line(i)
        slot = line if to else peer
        return pltpu.make_async_remote_copy(
            src_ref=part.at[source_rows(peer)],
            dst_ref=zbuf.at[slot],
            send_sem=zs_sem.at[peer],
            recv_sem=zr_sem.at[slot],
            device_id=device,
            device_id_type=MESH,
        )

    @pl.loop(1, LINE)
    def _(i):
        line_copy(i, True).start()

    zbuf[line] = part[source_rows(line)]

    @pl.loop(1, LINE)
    def _(i):
        line_copy(i, False).wait_recv()

    response = zbuf[0]
    for i in range(1, LINE):
        response = response + zbuf[i]
    rbuf[frq] = response.astype(jnp.bfloat16)

    def response_copy(i, to):
        peer, device = on_frq(i)
        slot = frq if to else peer
        return pltpu.make_async_remote_copy(
            src_ref=rbuf.at[frq],
            dst_ref=rbuf.at[slot],
            send_sem=rs_sem.at[peer],
            recv_sem=rr_sem.at[slot],
            device_id=device,
            device_id_type=MESH,
        )

    for i in range(1, GROUPS):
        response_copy(i, True).start()
    for i in range(1, GROUPS):
        response_copy(i, False).wait_recv()

    for j in range(GROUPS):
        terms = jnp.broadcast_to(rbuf[j].astype(jnp.float32)[None], (ROWS, RCV, LANES))
        own = iota((ROWS, RCV, LANES), 2) % ROWS == iota((ROWS, RCV, LANES), 0)
        lhs[:, j * LANES : (j + 1) * LANES] = (
            jnp.where(own, terms, 0.0).astype(jnp.bfloat16).reshape(ROWS * RCV, LANES)
        )
    traces_out = jnp.dot(lhs[...], texp[...], preferred_element_type=jnp.float32)
    out_ref[...] = (traces_out * (1.0 / math.sqrt(BAND_FREQUENCIES))).reshape(ROWS, RCV, TIME)

    @pl.loop(1, PLANE)
    def _(i):
        kernel_send(i).wait_send()
        spectra_copy(i, True).wait_send()

    @pl.loop(1, LINE)
    def _(i):
        line_copy(i, True).wait_send()

    for i in range(1, GROUPS):
        sums_copy(i, True).wait_send()
        response_copy(i, True).wait_send()


def per_device(traces, taper_start, taper_stop, freq_index, kernel):
    smem = pl.BlockSpec(memory_space=pltpu.SMEM)
    anywhere = pl.BlockSpec(memory_space=pl.ANY)
    dma = pltpu.SemaphoreType.DMA
    return pl.pallas_call(
        body,
        out_shape=jax.ShapeDtypeStruct((ROWS, RCV, TIME), jnp.float32),
        in_specs=[smem, smem, smem, anywhere, anywhere],
        out_specs=pl.BlockSpec(memory_space=pltpu.VMEM),
        scratch_shapes=[
            pltpu.VMEM((ROWS, RCV, TIME), jnp.bfloat16),
            pltpu.VMEM((2, FREQS, PLANE, RCV, SRC), jnp.bfloat16),
            pltpu.VMEM((GROUPS * FC, ROWS * RCV), jnp.float32),
            pltpu.VMEM((GROUPS, FC, ROWS * RCV), jnp.float32),
            pltpu.VMEM((PLANE, RCV, LANES), jnp.bfloat16),
            pltpu.VMEM((SRC, LANES), jnp.float32),
            pltpu.VMEM((LINE, RCV, LANES), jnp.float32),
            pltpu.VMEM((GROUPS, RCV, LANES), jnp.bfloat16),
            pltpu.VMEM((GROUPS * LANES, TIME), jnp.bfloat16),
            pltpu.VMEM((ROWS * RCV, GROUPS * LANES), jnp.bfloat16),
            dma((2,)),
            dma((PLANE,)),
            dma((PLANE,)),
            dma((GROUPS,)),
            dma((GROUPS,)),
            dma((PLANE,)),
            dma((PLANE,)),
            dma((LINE,)),
            dma((LINE,)),
            dma((GROUPS,)),
            dma((GROUPS,)),
        ],
        compiler_params=pltpu.CompilerParams(
            collective_id=0, has_side_effects=True, vmem_limit_bytes=32 * 1024 * 1024
        ),
        cost_estimate=pl.CostEstimate(
            flops=2 * 40_000_000, bytes_accessed=2 * 1024 * 1024, transcendentals=0
        ),
    )(taper_start, taper_stop, freq_index, traces, kernel)


def solution(mesh):
    in_specs = (P(None, "rcv", "frq"), P("rcv"), P("rcv"), P(), P(None, "frq", "rcv", None))
    out_specs = P(None, "rcv", "frq")
    return jax.shard_map(
        per_device, mesh=mesh, in_specs=in_specs, out_specs=out_specs, check_vma=False
    )
```

```python
import math

import jax
import jax.numpy as jnp
from jax import lax
from jax.experimental import pallas as pl
from jax.experimental.pallas import tpu as pltpu
from jax.sharding import PartitionSpec as P

BAND_FREQUENCIES = 16
PADDED_LENGTH = 3072
MESH = pl.DeviceIdType.MESH

ROWS = 32
RCV = 16
TIME = 512
FREQS = 4
PLANE = 16
LINE = 8
RING = 16
GROUPS = 4
FC = 2 * FREQS
LANES = FC * ROWS
SRC = 128
HALF = ROWS // 2
PLANE_STEPS = (
    (2, 2), (2, 1), (2, 3), (1, 2), (3, 2), (1, 1), (1, 3), (3, 1),
    (3, 3), (2, 0), (0, 2), (1, 0), (3, 0), (0, 1), (0, 3),
)
RING_STEPS = (8, 7, 9, 6, 10, 5, 11, 4, 12, 3, 13, 2, 14, 1, 15)


def iota(shape, axis):
    return lax.broadcasted_iota(jnp.int32, shape, axis)


def column(ref, count, shape):
    rows = shape[0]
    each = rows // count
    row = iota(shape, 0) // each
    out = jnp.full(shape, ref[0], jnp.int32)
    for i in range(1, count):
        out = jnp.where(row == i, ref[i], out)
    return out


def tables(freq_ref, first_sample):
    shape = (2 * BAND_FREQUENCIES, TIME)
    bins = column(freq_ref, BAND_FREQUENCIES, shape)
    steps = bins * (first_sample + iota(shape, 1)) + (iota(shape, 0) % 2) * (PADDED_LENGTH // 4)
    steps = steps.astype(jnp.float32)
    steps = steps - jnp.floor(steps * (1.0 / PADDED_LENGTH)) * PADDED_LENGTH
    steps = jnp.where(steps < 0, steps + PADDED_LENGTH, steps)
    steps = jnp.where(steps >= PADDED_LENGTH, steps - PADDED_LENGTH, steps)
    x = (jnp.abs(steps - PADDED_LENGTH // 2) - PADDED_LENGTH // 4) * (2.0 * math.pi / PADDED_LENGTH)
    y = x * x
    poly = jnp.full(shape, -1.0 / math.factorial(11), jnp.float32)
    for power in (9, 7, 5, 3, 1):
        sign = 1.0 if power % 4 == 1 else -1.0
        poly = poly * y + sign / math.factorial(power)
    return x * poly


def body(
    start_hbm,
    stop_hbm,
    freq_hbm,
    traces_ref,
    kernel_ref,
    response_ref,
    table_ref,
    start_ref,
    stop_ref,
    freq_ref,
    tr_buf,
    kbuf,
    pown,
    pbuf,
    fbuf,
    gbuf,
    part,
    pout,
    zbuf,
    rbuf,
    local_sem,
    ks_sem,
    kr_sem,
    fs_sem,
    fr_sem,
    gs_sem,
    gr_sem,
    zs_sem,
    zr_sem,
    rs_sem,
    rr_sem,
):
    rcv = lax.axis_index("rcv")
    frq = lax.axis_index("frq")
    plane = rcv // LINE
    line = rcv % LINE
    high = frq // 2
    core = frq % 2
    ring = high * LINE + line
    row = plane // 4
    col = plane % 4

    on_plane = []
    for across, down in PLANE_STEPS:
        peer = ((row + down) % 4) * 4 + (col + across) % 4
        on_plane.append((peer, (peer * LINE + line, frq)))
    on_ring = []
    for step in RING_STEPS:
        peer = (ring + step) % RING
        on_ring.append((peer, (plane * LINE + peer % LINE, (peer // LINE) * 2 + core)))
    sibling = (rcv, high * 2 + 1 - core)
    on_frq = [
        (peer, (rcv, peer))
        for peer in ((1 - high) * 2 + 1 - core, (1 - high) * 2 + core, high * 2 + 1 - core)
    ]

    barrier = pltpu.get_barrier_semaphore()
    greeted = on_ring + on_frq[:1] + on_frq[2:] + on_plane
    for _, device in greeted:
        pl.semaphore_signal(barrier, inc=1, device_id=device, device_id_type=MESH)

    traces_copy = pltpu.make_async_copy(traces_ref, tr_buf, local_sem.at[0])
    traces_copy.start()
    index_copies = [
        pltpu.make_async_copy(source, target, local_sem.at[2 + i])
        for i, (source, target) in enumerate(
            ((freq_hbm, freq_ref), (start_hbm, start_ref), (stop_hbm, stop_ref))
        )
    ]
    for copy in index_copies:
        copy.start()

    def columns(peer):
        return kernel_ref.at[:, :, :, pl.ds(pl.multiple_of(peer * SRC, SRC), SRC)]

    own_copy = pltpu.make_async_copy(columns(plane), kbuf.at[:, :, plane], local_sem.at[1])
    own_copy.start()

    for copy in index_copies:
        copy.wait()
    table = tables(freq_ref, frq * TIME).astype(jnp.bfloat16)

    sample = frq * TIME + iota((RCV, TIME), 1)
    start = column(start_ref, RCV, (RCV, TIME))
    stop = column(stop_ref, RCV, (RCV, TIME))
    window = jnp.where((sample >= start) & (sample < stop), 1.0, 0.0).astype(jnp.bfloat16)
    traces_copy.wait()
    tapered = (tr_buf[...] * window[None]).reshape(ROWS * RCV, TIME)
    sums = lax.dot_general(
        table, tapered, (((1,), (1,)), ((), ())), preferred_element_type=jnp.float32
    )
    for j in range(GROUPS):
        for half in range(2):
            piece = sums[j * FC : (j + 1) * FC, half * 256 : (half + 1) * 256]
            pown[j, half * FC : (half + 1) * FC] = piece
    pbuf[...] = pown[...].astype(jnp.bfloat16)

    pl.semaphore_wait(barrier, len(greeted))

    def sums_copy(to, slot, device):
        return pltpu.make_async_remote_copy(
            src_ref=pbuf.at[to],
            dst_ref=fbuf.at[slot],
            send_sem=fs_sem.at[to],
            recv_sem=fr_sem.at[slot],
            device_id=device,
            device_id_type=MESH,
        )

    for peer, device in on_frq:
        sums_copy(peer, frq, device).start()

    def kernel_copy(to, slot, device):
        return pltpu.make_async_remote_copy(
            src_ref=columns(to),
            dst_ref=kbuf.at[:, :, slot],
            send_sem=ks_sem.at[to],
            recv_sem=kr_sem.at[slot],
            device_id=device,
            device_id_type=MESH,
        )

    for peer, device in on_plane:
        kernel_copy(peer, plane, device).start()

    table_ref[...] = table

    total = pown[frq]
    for peer, device in on_frq:
        sums_copy(peer, peer, device).wait_recv()
    for peer, device in on_frq:
        total = total + fbuf[peer].astype(jnp.float32)
    total = total * (1.0 / math.sqrt(PADDED_LENGTH))
    spread = (FC, HALF, HALF * RCV)
    own_row = iota(spread, 2) // RCV == iota(spread, 1)
    pick = iota((RCV, HALF * RCV), 1) % RCV == iota((RCV, HALF * RCV), 0)
    pick = jnp.where(pick, 1.0, 0.0).astype(jnp.bfloat16)
    for half in range(2):
        wide = jnp.broadcast_to(total[half * FC : (half + 1) * FC][:, None, :], spread)
        wide = jnp.where(own_row, wide, 0.0).astype(jnp.bfloat16).reshape(FC * HALF, HALF * RCV)
        spectra = lax.dot_general(
            pick, wide, (((1,), (1,)), ((), ())), preferred_element_type=jnp.float32
        )
        gbuf[plane, :, half * 128 : (half + 1) * 128] = spectra.astype(jnp.bfloat16)

    def spectra_copy(to, slot, device):
        return pltpu.make_async_remote_copy(
            src_ref=gbuf.at[plane],
            dst_ref=gbuf.at[slot],
            send_sem=gs_sem.at[to],
            recv_sem=gr_sem.at[slot],
            device_id=device,
            device_id_type=MESH,
        )

    for peer, device in on_plane:
        spectra_copy(peer, plane, device).start()

    own_copy.wait()
    for peer, device in on_plane:
        kernel_copy(peer, peer, device).wait_recv()
    for peer, device in on_plane:
        spectra_copy(peer, peer, device).wait_recv()

    flipped = []
    for half in range(2):
        block = gbuf[:, :, half * 128 : (half + 1) * 128].reshape(PLANE * RCV, 128)
        flipped.append(block.astype(jnp.float32).T)
    for pair in range(FREQS // 2):
        halves = []
        for f in (pair * 2, pair * 2 + 1):
            at = f * 2 * HALF
            real = [block[at : at + HALF] for block in flipped]
            imag = [block[at + HALF : at + 2 * HALF] for block in flipped]
            left = jnp.concatenate(real + imag, axis=0).astype(jnp.bfloat16)
            right = jnp.concatenate(imag + [-block for block in real], axis=0).astype(jnp.bfloat16)
            halves.append(
                jnp.dot(
                    left, kbuf[0, f].reshape(PLANE * RCV, SRC), preferred_element_type=jnp.float32
                )
                + jnp.dot(
                    right, kbuf[1, f].reshape(PLANE * RCV, SRC), preferred_element_type=jnp.float32
                )
            )
        turned = jnp.concatenate(halves, axis=0).T
        part[:, pair * 128 : (pair + 1) * 128] = turned
        pout[:, pair * 128 : (pair + 1) * 128] = turned.astype(jnp.bfloat16)

    def source_rows(place):
        return pl.ds(pl.multiple_of((place % LINE) * RCV, RCV), RCV)

    def ring_copy(to, slot, device):
        return pltpu.make_async_remote_copy(
            src_ref=pout.at[source_rows(to)],
            dst_ref=zbuf.at[slot],
            send_sem=zs_sem.at[to],
            recv_sem=zr_sem.at[slot],
            device_id=device,
            device_id_type=MESH,
        )

    for peer, device in on_ring:
        ring_copy(peer, ring, device).start()

    zbuf[ring] = jnp.zeros((RCV, LANES), jnp.bfloat16)
    near = part[source_rows(ring)]
    far = jnp.zeros((RCV, LANES), jnp.float32)

    for peer, device in on_ring:
        ring_copy(peer, peer, device).wait_recv()

    for i in range(LINE):
        near = near + zbuf[high * LINE + i].astype(jnp.float32)
        far = far + zbuf[(1 - high) * LINE + i].astype(jnp.float32)
    rbuf[core, high] = near.astype(jnp.bfloat16)
    rbuf[core, 1 - high] = far.astype(jnp.bfloat16)

    def response_copy(slot):
        return pltpu.make_async_remote_copy(
            src_ref=rbuf.at[core],
            dst_ref=rbuf.at[slot],
            send_sem=rs_sem,
            recv_sem=rr_sem,
            device_id=sibling,
            device_id_type=MESH,
        )

    response_copy(core).start()
    response_copy(1 - core).wait_recv()
    for j in range(GROUPS):
        response_ref[j] = rbuf[j % 2, j // 2]

    for peer, device in on_plane:
        kernel_copy(peer, plane, device).wait_send()
        spectra_copy(peer, plane, device).wait_send()
    for peer, device in on_frq:
        sums_copy(peer, frq, device).wait_send()
    for peer, device in on_ring:
        ring_copy(peer, ring, device).wait_send()
    response_copy(core).wait_send()


def inverse(response_ref, table_ref, out_ref, texp, lhs):
    for i in range(2 * BAND_FREQUENCIES):
        texp[i * ROWS : (i + 1) * ROWS] = jnp.broadcast_to(table_ref[i : i + 1], (ROWS, TIME))
    for j in range(GROUPS):
        terms = jnp.broadcast_to(response_ref[j].astype(jnp.float32)[None], (ROWS, RCV, LANES))
        own = iota((ROWS, RCV, LANES), 2) % ROWS == iota((ROWS, RCV, LANES), 0)
        lhs[:, j * LANES : (j + 1) * LANES] = (
            jnp.where(own, terms, 0.0).astype(jnp.bfloat16).reshape(ROWS * RCV, LANES)
        )
    traces_out = jnp.dot(lhs[...], texp[...], preferred_element_type=jnp.float32)
    out_ref[...] = (traces_out * (1.0 / math.sqrt(BAND_FREQUENCIES))).reshape(ROWS, RCV, TIME)


def per_device(traces, taper_start, taper_stop, freq_index, kernel):
    vmem = pl.BlockSpec(memory_space=pltpu.VMEM)
    hbm = pl.BlockSpec(memory_space=pltpu.HBM)
    dma = pltpu.SemaphoreType.DMA
    response, table = pl.pallas_call(
        body,
        out_shape=[
            jax.ShapeDtypeStruct((GROUPS, RCV, LANES), jnp.bfloat16),
            jax.ShapeDtypeStruct((2 * BAND_FREQUENCIES, TIME), jnp.bfloat16),
        ],
        in_specs=[hbm] * 5,
        out_specs=[vmem] * 2,
        scratch_shapes=[
            pltpu.SMEM((RCV,), jnp.int32),
            pltpu.SMEM((RCV,), jnp.int32),
            pltpu.SMEM((BAND_FREQUENCIES,), jnp.int32),
            pltpu.VMEM((ROWS, RCV, TIME), jnp.bfloat16),
            pltpu.VMEM((2, FREQS, PLANE, RCV, SRC), jnp.bfloat16),
            pltpu.VMEM((GROUPS, 2 * FC, HALF * RCV), jnp.float32),
            pltpu.VMEM((GROUPS, 2 * FC, HALF * RCV), jnp.bfloat16),
            pltpu.VMEM((GROUPS, 2 * FC, HALF * RCV), jnp.bfloat16),
            pltpu.VMEM((PLANE, RCV, LANES), jnp.bfloat16),
            pltpu.VMEM((SRC, LANES), jnp.float32),
            pltpu.VMEM((SRC, LANES), jnp.bfloat16),
            pltpu.VMEM((RING, RCV, LANES), jnp.bfloat16),
            pltpu.VMEM((2, 2, RCV, LANES), jnp.bfloat16),
            dma((5,)),
            dma((PLANE,)),
            dma((PLANE,)),
            dma((GROUPS,)),
            dma((GROUPS,)),
            dma((PLANE,)),
            dma((PLANE,)),
            dma((RING,)),
            dma((RING,)),
            dma,
            dma,
        ],
        compiler_params=pltpu.CompilerParams(
            collective_id=0, has_side_effects=True, vmem_limit_bytes=60 * 1024 * 1024
        ),
        cost_estimate=pl.CostEstimate(
            flops=2 * 40_000_000, bytes_accessed=1024 * 1024, transcendentals=0
        ),
    )(taper_start, taper_stop, freq_index, traces, kernel)
    return pl.pallas_call(
        inverse,
        out_shape=jax.ShapeDtypeStruct((ROWS, RCV, TIME), jnp.float32),
        in_specs=[vmem] * 2,
        out_specs=vmem,
        scratch_shapes=[
            pltpu.VMEM((GROUPS * LANES, TIME), jnp.bfloat16),
            pltpu.VMEM((ROWS * RCV, GROUPS * LANES), jnp.bfloat16),
        ],
        compiler_params=pltpu.CompilerParams(vmem_limit_bytes=60 * 1024 * 1024),
        cost_estimate=pl.CostEstimate(
            flops=2 * 8_400_000, bytes_accessed=1024 * 1024, transcendentals=0
        ),
    )(response, table)


def solution(mesh):
    in_specs = (P(None, "rcv", "frq"), P("rcv"), P("rcv"), P(), P(None, "frq", "rcv", None))
    out_specs = P(None, "rcv", "frq")
    return jax.shard_map(
        per_device, mesh=mesh, in_specs=in_specs, out_specs=out_specs, check_vma=False
    )
```

```python
import math

import jax
import jax.numpy as jnp
from jax import lax
from jax.experimental import pallas as pl
from jax.experimental.pallas import tpu as pltpu
from jax.sharding import PartitionSpec as P

BAND_FREQUENCIES = 16
PADDED_LENGTH = 3072
MESH = pl.DeviceIdType.MESH

ROWS = 32
RCV = 16
TIME = 512
FREQS = 4
PLANE = 16
LINE = 8
RING = 16
GROUPS = 4
FC = 2 * FREQS
LANES = FC * ROWS
SRC = 128
HALF = ROWS // 2
PIECE = 256
PLANE_STEPS = (
    (2, 2), (2, 1), (2, 3), (1, 2), (3, 2), (1, 1), (1, 3), (3, 1),
    (3, 3), (2, 0), (0, 2), (1, 0), (3, 0), (0, 1), (0, 3),
)


def iota(shape, axis):
    return lax.broadcasted_iota(jnp.int32, shape, axis)


def column(ref, count, shape):
    rows = shape[0]
    each = rows // count
    row = iota(shape, 0) // each
    out = jnp.full(shape, ref[0], jnp.int32)
    for i in range(1, count):
        out = jnp.where(row == i, ref[i], out)
    return out


def tables(freq_ref, first_sample):
    shape = (2 * BAND_FREQUENCIES, TIME)
    bins = column(freq_ref, BAND_FREQUENCIES, shape)
    steps = bins * (first_sample + iota(shape, 1)) + (iota(shape, 0) % 2) * (PADDED_LENGTH // 4)
    steps = steps.astype(jnp.float32)
    steps = steps - jnp.floor(steps * (1.0 / PADDED_LENGTH)) * PADDED_LENGTH
    steps = jnp.where(steps < 0, steps + PADDED_LENGTH, steps)
    steps = jnp.where(steps >= PADDED_LENGTH, steps - PADDED_LENGTH, steps)
    x = (jnp.abs(steps - PADDED_LENGTH // 2) - PADDED_LENGTH // 4) * (2.0 * math.pi / PADDED_LENGTH)
    y = x * x
    poly = jnp.full(shape, -1.0 / math.factorial(11), jnp.float32)
    for power in (9, 7, 5, 3, 1):
        sign = 1.0 if power % 4 == 1 else -1.0
        poly = poly * y + sign / math.factorial(power)
    return x * poly


def body(
    start_hbm,
    stop_hbm,
    freq_hbm,
    traces_ref,
    kernel_ref,
    response_ref,
    table_ref,
    start_ref,
    stop_ref,
    freq_ref,
    tr_buf,
    kbuf,
    pown,
    pbuf,
    fbuf,
    gbuf,
    part,
    pout,
    zbuf,
    rbuf,
    table_buf,
    local_sem,
    ks_sem,
    kr_sem,
    fs_sem,
    fr_sem,
    gs_sem,
    gr_sem,
    zs_sem,
    zr_sem,
    rs_sem,
    rr_sem,
):
    rcv = lax.axis_index("rcv")
    frq = lax.axis_index("frq")
    plane = rcv // LINE
    line = rcv % LINE
    high = frq // 2
    core = frq % 2
    ring = high * LINE + line
    row = plane // 4
    col = plane % 4

    on_plane = []
    for across, down in PLANE_STEPS:
        peer = ((row + down) % 4) * 4 + (col + across) % 4
        on_plane.append((peer, (peer * LINE + line, frq)))
    on_ring = []
    for i in range(RING - 1):
        peer = i + (i + RING - ring) // RING
        on_ring.append((peer, (plane * LINE + peer % LINE, (peer // LINE) * 2 + core)))
    sibling = (rcv, high * 2 + 1 - core)
    on_frq = [
        (peer, (rcv, peer))
        for peer in ((1 - high) * 2 + 1 - core, (1 - high) * 2 + core, high * 2 + 1 - core)
    ]

    barrier = pltpu.get_barrier_semaphore()
    greeted = on_frq[:1] + on_ring + on_plane + on_frq[2:]
    for _, device in greeted:
        pl.semaphore_signal(barrier, inc=1, device_id=device, device_id_type=MESH)

    traces_copy = pltpu.make_async_copy(traces_ref, tr_buf, local_sem.at[0])
    traces_copy.start()
    index_copies = [
        pltpu.make_async_copy(source, target, local_sem.at[2 + i])
        for i, (source, target) in enumerate(
            ((freq_hbm, freq_ref), (start_hbm, start_ref), (stop_hbm, stop_ref))
        )
    ]
    for copy in index_copies:
        copy.start()

    def columns(peer):
        return kernel_ref.at[:, :, :, pl.ds(pl.multiple_of(peer * SRC, SRC), SRC)]

    own_copy = pltpu.make_async_copy(columns(plane), kbuf.at[:, :, plane], local_sem.at[1])
    own_copy.start()

    for copy in index_copies:
        copy.wait()
    table = tables(freq_ref, frq * TIME).astype(jnp.bfloat16)

    sample = frq * TIME + iota((RCV, TIME), 1)
    start = column(start_ref, RCV, (RCV, TIME))
    stop = column(stop_ref, RCV, (RCV, TIME))
    window = jnp.where((sample >= start) & (sample < stop), 1.0, 0.0).astype(jnp.bfloat16)
    traces_copy.wait()
    tapered = (tr_buf[...] * window[None]).reshape(ROWS * RCV, TIME)
    sums = lax.dot_general(
        table, tapered, (((1,), (1,)), ((), ())), preferred_element_type=jnp.float32
    )
    for j in range(GROUPS):
        for half in range(2):
            piece = sums[j * FC : (j + 1) * FC, half * 256 : (half + 1) * 256]
            pown[j, half * FC : (half + 1) * FC] = piece
    pbuf[...] = pown[...].astype(jnp.bfloat16)

    pl.semaphore_wait(barrier, len(greeted))

    def sums_copy(to, slot, device):
        return pltpu.make_async_remote_copy(
            src_ref=pbuf.at[to],
            dst_ref=fbuf.at[slot],
            send_sem=fs_sem.at[to],
            recv_sem=fr_sem.at[slot],
            device_id=device,
            device_id_type=MESH,
        )

    for peer, device in on_frq:
        sums_copy(peer, frq, device).start()

    def kernel_copy(to, slot, device):
        return pltpu.make_async_remote_copy(
            src_ref=columns(to),
            dst_ref=kbuf.at[:, :, slot],
            send_sem=ks_sem.at[to],
            recv_sem=kr_sem.at[slot],
            device_id=device,
            device_id_type=MESH,
        )

    for peer, device in on_plane:
        kernel_copy(peer, plane, device).start()

    table_buf[...] = table
    table_copy = pltpu.make_async_copy(table_buf, table_ref, local_sem.at[5])
    table_copy.start()

    total = pown[frq]
    for peer, device in on_frq:
        sums_copy(peer, peer, device).wait_recv()
    for peer, device in on_frq:
        total = total + fbuf[peer].astype(jnp.float32)
    total = total * (1.0 / math.sqrt(PADDED_LENGTH))
    spread = (FC, HALF, HALF * RCV)
    own_row = iota(spread, 2) // RCV == iota(spread, 1)
    pick = iota((RCV, HALF * RCV), 1) % RCV == iota((RCV, HALF * RCV), 0)
    pick = jnp.where(pick, 1.0, 0.0).astype(jnp.bfloat16)
    for half in range(2):
        wide = jnp.broadcast_to(total[half * FC : (half + 1) * FC][:, None, :], spread)
        wide = jnp.where(own_row, wide, 0.0).astype(jnp.bfloat16).reshape(FC * HALF, HALF * RCV)
        spectra = lax.dot_general(
            pick, wide, (((1,), (1,)), ((), ())), preferred_element_type=jnp.float32
        )
        gbuf[plane, :, half * 128 : (half + 1) * 128] = spectra.astype(jnp.bfloat16)

    def spectra_copy(to, slot, device):
        return pltpu.make_async_remote_copy(
            src_ref=gbuf.at[plane],
            dst_ref=gbuf.at[slot],
            send_sem=gs_sem.at[to],
            recv_sem=gr_sem.at[slot],
            device_id=device,
            device_id_type=MESH,
        )

    for peer, device in on_plane:
        spectra_copy(peer, plane, device).start()

    own_copy.wait()
    for peer, device in on_plane:
        kernel_copy(peer, peer, device).wait_recv()
    for peer, device in on_plane:
        spectra_copy(peer, peer, device).wait_recv()

    flipped = []
    for half in range(2):
        block = gbuf[:, :, half * 128 : (half + 1) * 128].reshape(PLANE * RCV, 128)
        flipped.append(block.astype(jnp.float32).T)
    for pair in range(FREQS // 2):
        halves = []
        for f in (pair * 2, pair * 2 + 1):
            at = f * 2 * HALF
            real = [block[at : at + HALF] for block in flipped]
            imag = [block[at + HALF : at + 2 * HALF] for block in flipped]
            left = jnp.concatenate(real + imag, axis=0).astype(jnp.bfloat16)
            right = jnp.concatenate(imag + [-block for block in real], axis=0).astype(jnp.bfloat16)
            halves.append(
                jnp.dot(
                    left, kbuf[0, f].reshape(PLANE * RCV, SRC), preferred_element_type=jnp.float32
                )
                + jnp.dot(
                    right, kbuf[1, f].reshape(PLANE * RCV, SRC), preferred_element_type=jnp.float32
                )
            )
        turned = jnp.concatenate(halves, axis=0).T
        part[:, pair * 128 : (pair + 1) * 128] = turned
        pout[:, pair * 128 : (pair + 1) * 128] = turned.astype(jnp.bfloat16)

    def source_rows(place):
        return pl.ds(pl.multiple_of((place % LINE) * RCV, RCV), RCV)

    def ring_copy(to, slot, device):
        return pltpu.make_async_remote_copy(
            src_ref=pout.at[source_rows(to)],
            dst_ref=zbuf.at[slot],
            send_sem=zs_sem.at[to],
            recv_sem=zr_sem.at[slot],
            device_id=device,
            device_id_type=MESH,
        )

    for peer, device in on_ring:
        ring_copy(peer, ring, device).start()

    zbuf[ring] = jnp.zeros((RCV, LANES), jnp.bfloat16)
    near = part[source_rows(ring)]
    far = jnp.zeros((RCV, LANES), jnp.float32)

    for peer, device in on_ring:
        ring_copy(peer, peer, device).wait_recv()

    for i in range(LINE):
        near = near + zbuf[high * LINE + i].astype(jnp.float32)
        far = far + zbuf[(1 - high) * LINE + i].astype(jnp.float32)
    rbuf[high] = near.astype(jnp.bfloat16)
    rbuf[1 - high] = far.astype(jnp.bfloat16)

    def response_copy(slot):
        return pltpu.make_async_remote_copy(
            src_ref=rbuf,
            dst_ref=response_ref.at[slot],
            send_sem=rs_sem,
            recv_sem=rr_sem,
            device_id=sibling,
            device_id_type=MESH,
        )

    response_copy(core).start()
    own_response = pltpu.make_async_copy(rbuf, response_ref.at[core], local_sem.at[6])
    own_response.start()

    for peer, device in on_plane:
        kernel_copy(peer, plane, device).wait_send()
        spectra_copy(peer, plane, device).wait_send()
    for peer, device in on_frq:
        sums_copy(peer, frq, device).wait_send()
    for peer, device in on_ring:
        ring_copy(peer, ring, device).wait_send()

    table_copy.wait()
    own_response.wait()
    response_copy(core).wait_send()
    response_copy(1 - core).wait_recv()


def inverse(response_hbm, table_hbm, out_hbm, response, table, texp, lhs, result, in_sem, out_sem):
    copies = [
        pltpu.make_async_copy(table_hbm, table, in_sem.at[0]),
        pltpu.make_async_copy(response_hbm, response, in_sem.at[1]),
    ]
    for copy in copies:
        copy.start()
    own = iota((8, RCV, 128), 2) % 8 == iota((8, RCV, 128), 0)
    own = jnp.where(own, 1.0, 0.0).astype(jnp.bfloat16)
    slot = iota((RCV, 128), 1) // 8 % 4
    copies[0].wait()
    for m in range(2):
        for q in range(4):
            for i in range(4):
                row = (4 * m + i) * 4 + q
                at = m * 128 + 32 * q + 8 * i
                texp[at : at + 8] = jnp.broadcast_to(table[row : row + 1], (8, TIME))
    copies[1].wait()
    for m in range(2):
        tiles = []
        for i in range(4):
            j, half = (4 * m + i) // 2, i % 2
            tile = response[j % 2, j // 2, :, half * 128 : (half + 1) * 128]
            tiles.append(tile.astype(jnp.float32))
        for a in range(ROWS // 8):
            merged = tiles[a]
            for i in range(4):
                if i != a:
                    turned = pltpu.roll(tiles[i], 8 * (i - a) % 128, 1)
                    merged = jnp.where(slot == i, turned, merged)
            terms = merged.astype(jnp.bfloat16)[None] * own
            lhs[a * 128 : (a + 1) * 128, m * 128 : (m + 1) * 128] = terms.reshape(128, 128)
    pieces = []
    for n in range(TIME // PIECE):
        samples = slice(n * PIECE, (n + 1) * PIECE)
        traces_out = jnp.dot(lhs[...], texp[:, samples], preferred_element_type=jnp.float32)
        traces_out = traces_out * (1.0 / math.sqrt(BAND_FREQUENCIES))
        result[n] = traces_out.reshape(ROWS, RCV, PIECE)
        pieces.append(
            pltpu.make_async_copy(result.at[n], out_hbm.at[:, :, samples], out_sem.at[n])
        )
        pieces[-1].start()
    for piece in pieces:
        piece.wait()


def per_device(traces, taper_start, taper_stop, freq_index, kernel):
    hbm = pl.BlockSpec(memory_space=pltpu.HBM)
    dma = pltpu.SemaphoreType.DMA
    response, table = pl.pallas_call(
        body,
        out_shape=[
            jax.ShapeDtypeStruct((2, 2, RCV, LANES), jnp.bfloat16),
            jax.ShapeDtypeStruct((2 * BAND_FREQUENCIES, TIME), jnp.bfloat16),
        ],
        in_specs=[hbm] * 5,
        out_specs=[hbm] * 2,
        scratch_shapes=[
            pltpu.SMEM((RCV,), jnp.int32),
            pltpu.SMEM((RCV,), jnp.int32),
            pltpu.SMEM((BAND_FREQUENCIES,), jnp.int32),
            pltpu.VMEM((ROWS, RCV, TIME), jnp.bfloat16),
            pltpu.VMEM((2, FREQS, PLANE, RCV, SRC), jnp.bfloat16),
            pltpu.VMEM((GROUPS, 2 * FC, HALF * RCV), jnp.float32),
            pltpu.VMEM((GROUPS, 2 * FC, HALF * RCV), jnp.bfloat16),
            pltpu.VMEM((GROUPS, 2 * FC, HALF * RCV), jnp.bfloat16),
            pltpu.VMEM((PLANE, RCV, LANES), jnp.bfloat16),
            pltpu.VMEM((SRC, LANES), jnp.float32),
            pltpu.VMEM((SRC, LANES), jnp.bfloat16),
            pltpu.VMEM((RING, RCV, LANES), jnp.bfloat16),
            pltpu.VMEM((2, RCV, LANES), jnp.bfloat16),
            pltpu.VMEM((2 * BAND_FREQUENCIES, TIME), jnp.bfloat16),
            dma((7,)),
            dma((PLANE,)),
            dma((PLANE,)),
            dma((GROUPS,)),
            dma((GROUPS,)),
            dma((PLANE,)),
            dma((PLANE,)),
            dma((RING,)),
            dma((RING,)),
            dma,
            dma,
        ],
        compiler_params=pltpu.CompilerParams(
            collective_id=0, has_side_effects=True, vmem_limit_bytes=60 * 1024 * 1024
        ),
        cost_estimate=pl.CostEstimate(
            flops=2 * 40_000_000, bytes_accessed=1024 * 1024, transcendentals=0
        ),
    )(taper_start, taper_stop, freq_index, traces, kernel)
    return pl.pallas_call(
        inverse,
        out_shape=jax.ShapeDtypeStruct((ROWS, RCV, TIME), jnp.float32),
        in_specs=[hbm] * 2,
        out_specs=hbm,
        scratch_shapes=[
            pltpu.VMEM((2, 2, RCV, LANES), jnp.bfloat16),
            pltpu.VMEM((2 * BAND_FREQUENCIES, TIME), jnp.bfloat16),
            pltpu.VMEM((256, TIME), jnp.bfloat16),
            pltpu.VMEM((ROWS * RCV, 256), jnp.bfloat16),
            pltpu.VMEM((TIME // PIECE, ROWS, RCV, PIECE), jnp.float32),
            dma((2,)),
            dma((TIME // PIECE,)),
        ],
        compiler_params=pltpu.CompilerParams(vmem_limit_bytes=60 * 1024 * 1024),
        cost_estimate=pl.CostEstimate(
            flops=2 * 8_400_000, bytes_accessed=1024 * 1024, transcendentals=0
        ),
    )(response, table)


def solution(mesh):
    in_specs = (P(None, "rcv", "frq"), P("rcv"), P("rcv"), P(), P(None, "frq", "rcv", None))
    out_specs = P(None, "rcv", "frq")
    return jax.shard_map(
        per_device, mesh=mesh, in_specs=in_specs, out_specs=out_specs, check_vma=False
    )
```

```python
import math

import jax
import jax.numpy as jnp
from jax import lax
from jax.experimental import pallas as pl
from jax.experimental.pallas import tpu as pltpu
from jax.sharding import PartitionSpec as P

BAND_FREQUENCIES = 16
PADDED_LENGTH = 3072
MESH = pl.DeviceIdType.MESH

ROWS = 32
RCV = 16
TIME = 512
FREQS = 4
PLANE = 16
LINE = 8
RING = 16
GROUPS = 4
FC = 2 * FREQS
LANES = FC * ROWS
SRC = 128
HALF = ROWS // 2
PIECE = 256
PLANE_STEPS = (
    (2, 2), (2, 1), (2, 3), (1, 2), (3, 2), (1, 1), (1, 3), (3, 1),
    (3, 3), (2, 0), (0, 2), (1, 0), (3, 0), (0, 1), (0, 3),
)


def iota(shape, axis):
    return lax.broadcasted_iota(jnp.int32, shape, axis)


def column(ref, count, shape):
    rows = shape[0]
    each = rows // count
    row = iota(shape, 0) // each
    out = jnp.full(shape, ref[0], jnp.int32)
    for i in range(1, count):
        out = jnp.where(row == i, ref[i], out)
    return out


def tables(freq_ref, first_sample):
    shape = (2 * BAND_FREQUENCIES, TIME)
    bins = column(freq_ref, BAND_FREQUENCIES, shape)
    steps = bins * (first_sample + iota(shape, 1)) + (iota(shape, 0) % 2) * (PADDED_LENGTH // 4)
    steps = steps.astype(jnp.float32)
    steps = steps - jnp.floor(steps * (1.0 / PADDED_LENGTH)) * PADDED_LENGTH
    steps = jnp.where(steps < 0, steps + PADDED_LENGTH, steps)
    steps = jnp.where(steps >= PADDED_LENGTH, steps - PADDED_LENGTH, steps)
    x = (jnp.abs(steps - PADDED_LENGTH // 2) - PADDED_LENGTH // 4) * (2.0 * math.pi / PADDED_LENGTH)
    y = x * x
    poly = jnp.full(shape, -1.0 / math.factorial(11), jnp.float32)
    for power in (9, 7, 5, 3, 1):
        sign = 1.0 if power % 4 == 1 else -1.0
        poly = poly * y + sign / math.factorial(power)
    return x * poly


def body(
    start_hbm,
    stop_hbm,
    freq_hbm,
    traces_ref,
    kernel_ref,
    response_ref,
    table_ref,
    start_ref,
    stop_ref,
    freq_ref,
    tr_buf,
    kbuf,
    pown,
    pside,
    pbuf,
    fbuf,
    gbuf,
    part,
    pout,
    zbuf,
    rbuf,
    table_buf,
    local_sem,
    ks_sem,
    kr_sem,
    side_sem,
    fs_sem,
    gs_sem,
    gr_sem,
    zs_sem,
    zr_sem,
    rs_sem,
):
    rcv = lax.axis_index("rcv")
    frq = lax.axis_index("frq")
    plane = rcv // LINE
    line = rcv % LINE
    high = frq // 2
    core = frq % 2
    ring = high * LINE + line
    row = plane // 4
    col = plane % 4

    on_plane = []
    for across, down in PLANE_STEPS:
        peer = ((row + down) % 4) * 4 + (col + across) % 4
        on_plane.append((peer, (peer * LINE + line, high * 2 + 1)))
    on_ring = []
    for i in range(RING - 1):
        peer = i + (i + RING - ring) // RING
        on_ring.append((peer, (plane * LINE + peer % LINE, (peer // LINE) * 2 + 1)))
    opposite = (rcv, (1 - high) * 2 + 1)
    sibling = (rcv, high * 2 + 1 - core)

    barrier = pltpu.get_barrier_semaphore()

    def greet(device):
        pl.semaphore_signal(barrier, inc=1, device_id=device, device_id_type=MESH)

    @pl.when(core == 1)
    def _():
        for _, device in on_ring + on_plane:
            greet(device)
        greet(sibling)
        for peer, _ in on_plane:
            greet((peer * LINE + line, high * 2))

    @pl.when(core == 0)
    def _():
        greet(sibling)

    traces_copy = pltpu.make_async_copy(traces_ref, tr_buf, local_sem.at[0])
    traces_copy.start()
    index_copies = [
        pltpu.make_async_copy(source, target, local_sem.at[2 + i])
        for i, (source, target) in enumerate(
            ((freq_hbm, freq_ref), (start_hbm, start_ref), (stop_hbm, stop_ref))
        )
    ]
    for copy in index_copies:
        copy.start()
    for copy in index_copies:
        copy.wait()
    table = tables(freq_ref, frq * TIME).astype(jnp.bfloat16)
    table_buf[...] = table
    table_copy = pltpu.make_async_copy(table_buf, table_ref, local_sem.at[5])
    table_copy.start()

    sample = frq * TIME + iota((RCV, TIME), 1)
    start = column(start_ref, RCV, (RCV, TIME))
    stop = column(stop_ref, RCV, (RCV, TIME))
    window = jnp.where((sample >= start) & (sample < stop), 1.0, 0.0).astype(jnp.bfloat16)
    traces_copy.wait()
    tapered = (tr_buf[...] * window[None]).reshape(ROWS * RCV, TIME)
    sums = lax.dot_general(
        table, tapered, (((1,), (1,)), ((), ())), preferred_element_type=jnp.float32
    )
    for j in range(GROUPS):
        for half in range(2):
            piece = sums[j * FC : (j + 1) * FC, half * 256 : (half + 1) * 256]
            pown[j, half * FC : (half + 1) * FC] = piece

    def columns(peer):
        return kernel_ref.at[:, :, :, pl.ds(pl.multiple_of(peer * SRC, SRC), SRC)]

    def remote(source, target, send_sem, recv_sem, device):
        return pltpu.make_async_remote_copy(
            src_ref=source,
            dst_ref=target,
            send_sem=send_sem,
            recv_sem=recv_sem,
            device_id=device,
            device_id_type=MESH,
        )

    def kernel_copy(group, to, slot, device):
        return remote(
            columns(to), kbuf.at[group, :, :, slot], ks_sem.at[to], kr_sem.at[group, slot], device
        )

    side_copy = remote(pown, pside, side_sem.at[0], side_sem.at[1], sibling)
    response_copy = remote(rbuf, response_ref, rs_sem.at[0], rs_sem.at[1], sibling)

    @pl.when(core == 0)
    def _():
        pl.semaphore_wait(barrier, PLANE)
        side_copy.start()
        for peer, device in on_plane:
            kernel_copy(0, peer, plane, device).start()
        kernel_copy(0, plane, plane, sibling).start()
        side_copy.wait_send()
        for peer, device in on_plane:
            kernel_copy(0, peer, plane, device).wait_send()
        kernel_copy(0, plane, plane, sibling).wait_send()
        response_copy.wait_recv()

    @pl.when(core == 1)
    def _():
        own_copy = pltpu.make_async_copy(
            columns(plane), kbuf.at[1, :, :, plane], local_sem.at[1]
        )
        own_copy.start()

        side_copy.wait_recv()
        for j in range(GROUPS):
            pown[j] = pown[j] + pside[j]
        for c in range(2):
            pbuf[c] = pown[(1 - high) * 2 + c].astype(jnp.bfloat16)

        pl.semaphore_wait(barrier, PLANE + RING - 1)

        sums_copy = remote(pbuf, fbuf, fs_sem.at[0], fs_sem.at[1], opposite)
        sums_copy.start()
        for peer, device in on_plane:
            kernel_copy(1, peer, plane, device).start()

        spread = (FC, HALF, HALF * RCV)
        own_row = iota(spread, 2) // RCV == iota(spread, 1)
        pick = iota((RCV, HALF * RCV), 1) % RCV == iota((RCV, HALF * RCV), 0)
        pick = jnp.where(pick, 1.0, 0.0).astype(jnp.bfloat16)
        sums_copy.wait_recv()
        for c in range(2):
            total = pown[high * 2 + c] + fbuf[c].astype(jnp.float32)
            total = total * (1.0 / math.sqrt(PADDED_LENGTH))
            for half in range(2):
                wide = jnp.broadcast_to(total[half * FC : (half + 1) * FC][:, None, :], spread)
                wide = jnp.where(own_row, wide, 0.0).astype(jnp.bfloat16)
                spectra = lax.dot_general(
                    pick,
                    wide.reshape(FC * HALF, HALF * RCV),
                    (((1,), (1,)), ((), ())),
                    preferred_element_type=jnp.float32,
                )
                at = c * LANES + half * 128
                gbuf[plane, :, at : at + 128] = spectra.astype(jnp.bfloat16)

        def spectra_copy(to, slot, device):
            return remote(gbuf.at[plane], gbuf.at[slot], gs_sem.at[to], gr_sem.at[slot], device)

        for peer, device in on_plane:
            spectra_copy(peer, plane, device).start()

        own_copy.wait()
        kernel_copy(0, plane, plane, sibling).wait_recv()
        for peer, device in on_plane:
            kernel_copy(0, peer, peer, device).wait_recv()
            kernel_copy(1, peer, peer, device).wait_recv()
        for peer, device in on_plane:
            spectra_copy(peer, peer, device).wait_recv()

        for group in range(2):
            flipped = []
            for half in range(2):
                at = group * LANES + half * 128
                block = gbuf[:, :, at : at + 128].reshape(PLANE * RCV, 128)
                flipped.append(block.astype(jnp.float32).T)
            for pair in range(FREQS // 2):
                halves = []
                for f in (pair * 2, pair * 2 + 1):
                    at = f * 2 * HALF
                    real = [block[at : at + HALF] for block in flipped]
                    imag = [block[at + HALF : at + 2 * HALF] for block in flipped]
                    left = jnp.concatenate(real + imag, axis=0).astype(jnp.bfloat16)
                    right = jnp.concatenate(imag + [-block for block in real], axis=0)
                    right = right.astype(jnp.bfloat16)
                    halves.append(
                        jnp.dot(
                            left,
                            kbuf[group, 0, f].reshape(PLANE * RCV, SRC),
                            preferred_element_type=jnp.float32,
                        )
                        + jnp.dot(
                            right,
                            kbuf[group, 1, f].reshape(PLANE * RCV, SRC),
                            preferred_element_type=jnp.float32,
                        )
                    )
                turned = jnp.concatenate(halves, axis=0).T
                at = group * LANES + pair * 128
                part[:, at : at + 128] = turned
                pout[:, at : at + 128] = turned.astype(jnp.bfloat16)

        def source_rows(place):
            return pl.ds(pl.multiple_of((place % LINE) * RCV, RCV), RCV)

        def ring_copy(to, slot, device):
            return remote(
                pout.at[source_rows(to)], zbuf.at[slot], zs_sem.at[to], zr_sem.at[slot], device
            )

        for peer, device in on_ring:
            ring_copy(peer, ring, device).start()

        zbuf[ring] = jnp.zeros((RCV, 2 * LANES), jnp.bfloat16)
        near = part[source_rows(ring)]
        far = jnp.zeros((RCV, 2 * LANES), jnp.float32)

        for peer, device in on_plane:
            kernel_copy(1, peer, plane, device).wait_send()
            spectra_copy(peer, plane, device).wait_send()
        sums_copy.wait_send()
        for peer, device in on_ring:
            ring_copy(peer, peer, device).wait_recv()

        for i in range(LINE):
            near = near + zbuf[high * LINE + i].astype(jnp.float32)
            far = far + zbuf[(1 - high) * LINE + i].astype(jnp.float32)
        rbuf[high] = near.astype(jnp.bfloat16)
        rbuf[1 - high] = far.astype(jnp.bfloat16)

        own_response = pltpu.make_async_copy(rbuf, response_ref, local_sem.at[6])
        own_response.start()
        response_copy.start()
        for peer, device in on_ring:
            ring_copy(peer, ring, device).wait_send()
        own_response.wait()
        response_copy.wait_send()

    table_copy.wait()


def inverse(response_hbm, table_hbm, out_hbm, response, table, texp, lhs, result, in_sem, out_sem):
    copies = [
        pltpu.make_async_copy(table_hbm, table, in_sem.at[0]),
        pltpu.make_async_copy(response_hbm, response, in_sem.at[1]),
    ]
    for copy in copies:
        copy.start()
    own = iota((8, RCV, 128), 2) % 8 == iota((8, RCV, 128), 0)
    own = jnp.where(own, 1.0, 0.0).astype(jnp.bfloat16)
    slot = iota((RCV, 128), 1) // 8 % 4
    copies[0].wait()
    for m in range(2):
        for q in range(4):
            for i in range(4):
                row = (4 * m + i) * 4 + q
                at = m * 128 + 32 * q + 8 * i
                texp[at : at + 8] = jnp.broadcast_to(table[row : row + 1], (8, TIME))
    copies[1].wait()
    for m in range(2):
        tiles = []
        for i in range(4):
            tiles.append(response[m, :, i * 128 : (i + 1) * 128].astype(jnp.float32))
        for a in range(ROWS // 8):
            merged = tiles[a]
            for i in range(4):
                if i != a:
                    turned = pltpu.roll(tiles[i], 8 * (i - a) % 128, 1)
                    merged = jnp.where(slot == i, turned, merged)
            terms = merged.astype(jnp.bfloat16)[None] * own
            lhs[a * 128 : (a + 1) * 128, m * 128 : (m + 1) * 128] = terms.reshape(128, 128)
    pieces = []
    for n in range(TIME // PIECE):
        samples = slice(n * PIECE, (n + 1) * PIECE)
        traces_out = jnp.dot(lhs[...], texp[:, samples], preferred_element_type=jnp.float32)
        traces_out = traces_out * (1.0 / math.sqrt(BAND_FREQUENCIES))
        result[n] = traces_out.reshape(ROWS, RCV, PIECE)
        pieces.append(
            pltpu.make_async_copy(result.at[n], out_hbm.at[:, :, samples], out_sem.at[n])
        )
        pieces[-1].start()
    for piece in pieces:
        piece.wait()


def per_device(traces, taper_start, taper_stop, freq_index, kernel):
    hbm = pl.BlockSpec(memory_space=pltpu.HBM)
    dma = pltpu.SemaphoreType.DMA
    response, table = pl.pallas_call(
        body,
        out_shape=[
            jax.ShapeDtypeStruct((2, RCV, 2 * LANES), jnp.bfloat16),
            jax.ShapeDtypeStruct((2 * BAND_FREQUENCIES, TIME), jnp.bfloat16),
        ],
        in_specs=[hbm] * 5,
        out_specs=[hbm] * 2,
        scratch_shapes=[
            pltpu.SMEM((RCV,), jnp.int32),
            pltpu.SMEM((RCV,), jnp.int32),
            pltpu.SMEM((BAND_FREQUENCIES,), jnp.int32),
            pltpu.VMEM((ROWS, RCV, TIME), jnp.bfloat16),
            pltpu.VMEM((2, 2, FREQS, PLANE, RCV, SRC), jnp.bfloat16),
            pltpu.VMEM((GROUPS, 2 * FC, HALF * RCV), jnp.float32),
            pltpu.VMEM((GROUPS, 2 * FC, HALF * RCV), jnp.float32),
            pltpu.VMEM((2, 2 * FC, HALF * RCV), jnp.bfloat16),
            pltpu.VMEM((2, 2 * FC, HALF * RCV), jnp.bfloat16),
            pltpu.VMEM((PLANE, RCV, 2 * LANES), jnp.bfloat16),
            pltpu.VMEM((SRC, 2 * LANES), jnp.float32),
            pltpu.VMEM((SRC, 2 * LANES), jnp.bfloat16),
            pltpu.VMEM((RING, RCV, 2 * LANES), jnp.bfloat16),
            pltpu.VMEM((2, RCV, 2 * LANES), jnp.bfloat16),
            pltpu.VMEM((2 * BAND_FREQUENCIES, TIME), jnp.bfloat16),
            dma((7,)),
            dma((PLANE,)),
            dma((2, PLANE)),
            dma((2,)),
            dma((2,)),
            dma((PLANE,)),
            dma((PLANE,)),
            dma((RING,)),
            dma((RING,)),
            dma((2,)),
        ],
        compiler_params=pltpu.CompilerParams(
            collective_id=0, has_side_effects=True, vmem_limit_bytes=60 * 1024 * 1024
        ),
        cost_estimate=pl.CostEstimate(
            flops=2 * 40_000_000, bytes_accessed=1024 * 1024, transcendentals=0
        ),
    )(taper_start, taper_stop, freq_index, traces, kernel)
    return pl.pallas_call(
        inverse,
        out_shape=jax.ShapeDtypeStruct((ROWS, RCV, TIME), jnp.float32),
        in_specs=[hbm] * 2,
        out_specs=hbm,
        scratch_shapes=[
            pltpu.VMEM((2, RCV, 2 * LANES), jnp.bfloat16),
            pltpu.VMEM((2 * BAND_FREQUENCIES, TIME), jnp.bfloat16),
            pltpu.VMEM((256, TIME), jnp.bfloat16),
            pltpu.VMEM((ROWS * RCV, 256), jnp.bfloat16),
            pltpu.VMEM((TIME // PIECE, ROWS, RCV, PIECE), jnp.float32),
            dma((2,)),
            dma((TIME // PIECE,)),
        ],
        compiler_params=pltpu.CompilerParams(vmem_limit_bytes=60 * 1024 * 1024),
        cost_estimate=pl.CostEstimate(
            flops=2 * 8_400_000, bytes_accessed=1024 * 1024, transcendentals=0
        ),
    )(response, table)


def solution(mesh):
    in_specs = (P(None, "rcv", "frq"), P("rcv"), P("rcv"), P(), P(None, "frq", "rcv", None))
    out_specs = P(None, "rcv", "frq")
    return jax.shard_map(
        per_device, mesh=mesh, in_specs=in_specs, out_specs=out_specs, check_vma=False
    )
```

```python
import math

import jax
import jax.numpy as jnp
from jax import lax
from jax.experimental import pallas as pl
from jax.experimental.pallas import tpu as pltpu
from jax.sharding import PartitionSpec as P

BAND_FREQUENCIES = 16
PADDED_LENGTH = 3072
MESH = pl.DeviceIdType.MESH

ROWS = 32
RCV = 16
TIME = 512
FREQS = 4
PLANE = 16
LINE = 8
RING = 16
GROUPS = 4
FC = 2 * FREQS
LANES = FC * ROWS
SRC = 128
HALF = ROWS // 2
PIECE = 256
PLANE_STEPS = (
    (2, 2), (2, 1), (2, 3), (1, 2), (3, 2), (1, 1), (1, 3), (3, 1),
    (3, 3), (2, 0), (0, 2), (1, 0), (3, 0), (0, 1), (0, 3),
)


def iota(shape, axis):
    return lax.broadcasted_iota(jnp.int32, shape, axis)


def column(ref, count, shape):
    rows = shape[0]
    each = rows // count
    row = iota(shape, 0) // each
    out = jnp.full(shape, ref[0], jnp.int32)
    for i in range(1, count):
        out = jnp.where(row == i, ref[i], out)
    return out


def tables(freq_ref, first_sample):
    shape = (2 * BAND_FREQUENCIES, TIME)
    bins = column(freq_ref, BAND_FREQUENCIES, shape)
    steps = bins * (first_sample + iota(shape, 1)) + (iota(shape, 0) % 2) * (PADDED_LENGTH // 4)
    steps = steps.astype(jnp.float32)
    steps = steps - jnp.floor(steps * (1.0 / PADDED_LENGTH)) * PADDED_LENGTH
    steps = jnp.where(steps < 0, steps + PADDED_LENGTH, steps)
    steps = jnp.where(steps >= PADDED_LENGTH, steps - PADDED_LENGTH, steps)
    x = (jnp.abs(steps - PADDED_LENGTH // 2) - PADDED_LENGTH // 4) * (2.0 * math.pi / PADDED_LENGTH)
    y = x * x
    poly = jnp.full(shape, -1.0 / math.factorial(11), jnp.float32)
    for power in (9, 7, 5, 3, 1):
        sign = 1.0 if power % 4 == 1 else -1.0
        poly = poly * y + sign / math.factorial(power)
    return x * poly


def body(
    start_hbm,
    stop_hbm,
    freq_hbm,
    traces_ref,
    kernel_ref,
    response_ref,
    table_ref,
    start_ref,
    stop_ref,
    freq_ref,
    tr_buf,
    kbuf,
    pown,
    pside,
    pbuf,
    fbuf,
    gbuf,
    part,
    pout,
    zbuf,
    rbuf,
    table_buf,
    local_sem,
    ks_sem,
    kr_sem,
    side_sem,
    fs_sem,
    gs_sem,
    gr_sem,
    zs_sem,
    zr_sem,
    rs_sem,
):
    rcv = lax.axis_index("rcv")
    frq = lax.axis_index("frq")
    plane = rcv // LINE
    line = rcv % LINE
    high = frq // 2
    core = frq % 2
    ring = high * LINE + line
    row = plane // 4
    col = plane % 4

    on_plane = []
    for across, down in PLANE_STEPS:
        peer = ((row + down) % 4) * 4 + (col + across) % 4
        on_plane.append((peer, (peer * LINE + line, high * 2 + 1)))
    on_ring = []
    for i in range(RING - 1):
        peer = i + (i + RING - ring) // RING
        on_ring.append((peer, (plane * LINE + peer % LINE, (peer // LINE) * 2 + 1)))
    opposite = (rcv, (1 - high) * 2 + 1)
    sibling = (rcv, high * 2 + 1 - core)

    barrier = pltpu.get_barrier_semaphore()

    def greet(device):
        pl.semaphore_signal(barrier, inc=1, device_id=device, device_id_type=MESH)

    @pl.when(core == 1)
    def _():
        for _, device in on_ring + on_plane:
            greet(device)
        greet(sibling)
        for peer, _ in on_plane:
            greet((peer * LINE + line, high * 2))

    @pl.when(core == 0)
    def _():
        greet(sibling)

    traces_copy = pltpu.make_async_copy(traces_ref, tr_buf, local_sem.at[0])
    traces_copy.start()
    index_copies = [
        pltpu.make_async_copy(source, target, local_sem.at[2 + i])
        for i, (source, target) in enumerate(
            ((freq_hbm, freq_ref), (start_hbm, start_ref), (stop_hbm, stop_ref))
        )
    ]
    for copy in index_copies:
        copy.start()
    for copy in index_copies:
        copy.wait()
    table = tables(freq_ref, frq * TIME).astype(jnp.bfloat16)
    table_buf[...] = table
    table_copy = pltpu.make_async_copy(table_buf, table_ref, local_sem.at[5])
    table_copy.start()

    sample = frq * TIME + iota((RCV, TIME), 1)
    start = column(start_ref, RCV, (RCV, TIME))
    stop = column(stop_ref, RCV, (RCV, TIME))
    window = jnp.where((sample >= start) & (sample < stop), 1.0, 0.0).astype(jnp.bfloat16)
    traces_copy.wait()
    tapered = (tr_buf[...] * window[None]).reshape(ROWS * RCV, TIME)
    sums = lax.dot_general(
        table, tapered, (((1,), (1,)), ((), ())), preferred_element_type=jnp.float32
    )
    for j in range(GROUPS):
        for half in range(2):
            piece = sums[j * FC : (j + 1) * FC, half * 256 : (half + 1) * 256]
            pown[j, half * FC : (half + 1) * FC] = piece

    def columns(peer):
        return kernel_ref.at[:, :, :, pl.ds(pl.multiple_of(peer * SRC, SRC), SRC)]

    def remote(source, target, send_sem, recv_sem, device):
        return pltpu.make_async_remote_copy(
            src_ref=source,
            dst_ref=target,
            send_sem=send_sem,
            recv_sem=recv_sem,
            device_id=device,
            device_id_type=MESH,
        )

    def kernel_copy(group, to, slot, device):
        return remote(
            columns(to), kbuf.at[group, :, :, slot], ks_sem.at[to], kr_sem.at[group, slot], device
        )

    side_copy = remote(pown, pside, side_sem.at[0], side_sem.at[1], sibling)
    response_copy = remote(rbuf, response_ref, rs_sem.at[0], rs_sem.at[1], sibling)

    @pl.when(core == 0)
    def _():
        pl.semaphore_wait(barrier, PLANE)
        side_copy.start()
        for peer, device in on_plane:
            kernel_copy(0, peer, plane, device).start()
        kernel_copy(0, plane, plane, sibling).start()
        side_copy.wait_send()
        for peer, device in on_plane:
            kernel_copy(0, peer, plane, device).wait_send()
        kernel_copy(0, plane, plane, sibling).wait_send()
        response_copy.wait_recv()

    @pl.when(core == 1)
    def _():
        own_copy = pltpu.make_async_copy(
            columns(plane), kbuf.at[1, :, :, plane], local_sem.at[1]
        )
        own_copy.start()

        side_copy.wait_recv()
        for j in range(GROUPS):
            pown[j] = pown[j] + pside[j]
        for c in range(2):
            pbuf[c] = pown[(1 - high) * 2 + c].astype(jnp.bfloat16)

        pl.semaphore_wait(barrier, PLANE + RING - 1)

        sums_copy = remote(pbuf, fbuf, fs_sem.at[0], fs_sem.at[1], opposite)
        sums_copy.start()
        for peer, device in on_plane:
            kernel_copy(1, peer, plane, device).start()

        spread = (FC, HALF, HALF * RCV)
        own_row = iota(spread, 2) // RCV == iota(spread, 1)
        pick = iota((RCV, HALF * RCV), 1) % RCV == iota((RCV, HALF * RCV), 0)
        pick = jnp.where(pick, 1.0, 0.0).astype(jnp.bfloat16)
        sums_copy.wait_recv()
        for c in range(2):
            total = pown[high * 2 + c] + fbuf[c].astype(jnp.float32)
            total = total * (1.0 / math.sqrt(PADDED_LENGTH))
            for half in range(2):
                wide = jnp.broadcast_to(total[half * FC : (half + 1) * FC][:, None, :], spread)
                wide = jnp.where(own_row, wide, 0.0).astype(jnp.bfloat16)
                spectra = lax.dot_general(
                    pick,
                    wide.reshape(FC * HALF, HALF * RCV),
                    (((1,), (1,)), ((), ())),
                    preferred_element_type=jnp.float32,
                )
                at = c * LANES + half * 128
                gbuf[plane, :, at : at + 128] = spectra.astype(jnp.bfloat16)

        def spectra_copy(to, slot, device):
            return remote(gbuf.at[plane], gbuf.at[slot], gs_sem.at[to], gr_sem.at[slot], device)

        for peer, device in on_plane:
            spectra_copy(peer, plane, device).start()

        own_copy.wait()
        kernel_copy(0, plane, plane, sibling).wait_recv()
        for peer, device in on_plane:
            kernel_copy(0, peer, peer, device).wait_recv()
            kernel_copy(1, peer, peer, device).wait_recv()
        for peer, device in on_plane:
            spectra_copy(peer, peer, device).wait_recv()

        for group in range(2):
            flipped = []
            for half in range(2):
                at = group * LANES + half * 128
                block = gbuf[:, :, at : at + 128].reshape(PLANE * RCV, 128)
                flipped.append(block.astype(jnp.float32).T)
            for pair in range(FREQS // 2):
                halves = []
                for f in (pair * 2, pair * 2 + 1):
                    at = f * 2 * HALF
                    real = [block[at : at + HALF] for block in flipped]
                    imag = [block[at + HALF : at + 2 * HALF] for block in flipped]
                    left = jnp.concatenate(real + imag, axis=0).astype(jnp.bfloat16)
                    right = jnp.concatenate(imag + [-block for block in real], axis=0)
                    right = right.astype(jnp.bfloat16)
                    halves.append(
                        jnp.dot(
                            left,
                            kbuf[group, 0, f].reshape(PLANE * RCV, SRC),
                            preferred_element_type=jnp.float32,
                        )
                        + jnp.dot(
                            right,
                            kbuf[group, 1, f].reshape(PLANE * RCV, SRC),
                            preferred_element_type=jnp.float32,
                        )
                    )
                turned = jnp.concatenate(halves, axis=0).T
                at = group * LANES + pair * 128
                part[:, at : at + 128] = turned
                pout[:, at : at + 128] = turned.astype(jnp.bfloat16)

        def source_rows(place):
            return pl.ds(pl.multiple_of((place % LINE) * RCV, RCV), RCV)

        def ring_copy(to, slot, device):
            return remote(
                pout.at[source_rows(to)], zbuf.at[slot], zs_sem.at[to], zr_sem.at[slot], device
            )

        for peer, device in on_ring:
            ring_copy(peer, ring, device).start()

        near = part[source_rows(ring)]
        far = jnp.zeros((RCV, 2 * LANES), jnp.float32)

        for peer, device in on_plane:
            kernel_copy(1, peer, plane, device).wait_send()
            spectra_copy(peer, plane, device).wait_send()
        sums_copy.wait_send()
        for step in range(1, LINE):
            peer = high * LINE + (line + step) % LINE
            ring_copy(peer, peer, opposite).wait_recv()
            near = near + zbuf[peer].astype(jnp.float32)
        for step in range(LINE):
            peer = (1 - high) * LINE + (line + LINE - 1 - step) % LINE
            ring_copy(peer, peer, opposite).wait_recv()
            far = far + zbuf[peer].astype(jnp.float32)
        rbuf[high] = near.astype(jnp.bfloat16)
        rbuf[1 - high] = far.astype(jnp.bfloat16)

        own_response = pltpu.make_async_copy(rbuf, response_ref, local_sem.at[6])
        own_response.start()
        response_copy.start()
        for peer, device in on_ring:
            ring_copy(peer, ring, device).wait_send()
        own_response.wait()
        response_copy.wait_send()

    table_copy.wait()


def inverse(response_hbm, table_hbm, out_hbm, response, table, texp, lhs, result, in_sem, out_sem):
    copies = [
        pltpu.make_async_copy(table_hbm, table, in_sem.at[0]),
        pltpu.make_async_copy(response_hbm, response, in_sem.at[1]),
    ]
    for copy in copies:
        copy.start()
    own = iota((8, RCV, 128), 2) % 8 == iota((8, RCV, 128), 0)
    own = jnp.where(own, 1.0, 0.0).astype(jnp.bfloat16)
    slot = iota((RCV, 128), 1) // 8 % 4
    copies[0].wait()
    rows = table[...].astype(jnp.float32)
    for m in range(2):
        for q in range(4):
            block = []
            for i in range(4):
                row = (4 * m + i) * 4 + q
                block.append(jnp.broadcast_to(rows[row : row + 1], (8, TIME)))
            at = m * 128 + 32 * q
            texp[at : at + 32] = jnp.concatenate(block, axis=0).astype(jnp.bfloat16)
    copies[1].wait()
    for m in range(2):
        tiles = []
        for i in range(4):
            tiles.append(response[m, :, i * 128 : (i + 1) * 128].astype(jnp.float32))
        for a in range(ROWS // 8):
            merged = tiles[a]
            for i in range(4):
                if i != a:
                    turned = pltpu.roll(tiles[i], 8 * (i - a) % 128, 1)
                    merged = jnp.where(slot == i, turned, merged)
            terms = merged.astype(jnp.bfloat16)[None] * own
            lhs[a * 128 : (a + 1) * 128, m * 128 : (m + 1) * 128] = terms.reshape(128, 128)
    pieces = []
    for n in range(TIME // PIECE):
        samples = slice(n * PIECE, (n + 1) * PIECE)
        traces_out = jnp.dot(lhs[...], texp[:, samples], preferred_element_type=jnp.float32)
        traces_out = traces_out * (1.0 / math.sqrt(BAND_FREQUENCIES))
        result[n] = traces_out.reshape(ROWS, RCV, PIECE)
        pieces.append(
            pltpu.make_async_copy(result.at[n], out_hbm.at[:, :, samples], out_sem.at[n])
        )
        pieces[-1].start()
    for piece in pieces:
        piece.wait()


def per_device(traces, taper_start, taper_stop, freq_index, kernel):
    hbm = pl.BlockSpec(memory_space=pltpu.HBM)
    dma = pltpu.SemaphoreType.DMA
    response, table = pl.pallas_call(
        body,
        out_shape=[
            jax.ShapeDtypeStruct((2, RCV, 2 * LANES), jnp.bfloat16),
            jax.ShapeDtypeStruct((2 * BAND_FREQUENCIES, TIME), jnp.bfloat16),
        ],
        in_specs=[hbm] * 5,
        out_specs=[hbm] * 2,
        scratch_shapes=[
            pltpu.SMEM((RCV,), jnp.int32),
            pltpu.SMEM((RCV,), jnp.int32),
            pltpu.SMEM((BAND_FREQUENCIES,), jnp.int32),
            pltpu.VMEM((ROWS, RCV, TIME), jnp.bfloat16),
            pltpu.VMEM((2, 2, FREQS, PLANE, RCV, SRC), jnp.bfloat16),
            pltpu.VMEM((GROUPS, 2 * FC, HALF * RCV), jnp.float32),
            pltpu.VMEM((GROUPS, 2 * FC, HALF * RCV), jnp.float32),
            pltpu.VMEM((2, 2 * FC, HALF * RCV), jnp.bfloat16),
            pltpu.VMEM((2, 2 * FC, HALF * RCV), jnp.bfloat16),
            pltpu.VMEM((PLANE, RCV, 2 * LANES), jnp.bfloat16),
            pltpu.VMEM((SRC, 2 * LANES), jnp.float32),
            pltpu.VMEM((SRC, 2 * LANES), jnp.bfloat16),
            pltpu.VMEM((RING, RCV, 2 * LANES), jnp.bfloat16),
            pltpu.VMEM((2, RCV, 2 * LANES), jnp.bfloat16),
            pltpu.VMEM((2 * BAND_FREQUENCIES, TIME), jnp.bfloat16),
            dma((7,)),
            dma((PLANE,)),
            dma((2, PLANE)),
            dma((2,)),
            dma((2,)),
            dma((PLANE,)),
            dma((PLANE,)),
            dma((RING,)),
            dma((RING,)),
            dma((2,)),
        ],
        compiler_params=pltpu.CompilerParams(
            collective_id=0, has_side_effects=True, vmem_limit_bytes=60 * 1024 * 1024
        ),
        cost_estimate=pl.CostEstimate(
            flops=2 * 40_000_000, bytes_accessed=1024 * 1024, transcendentals=0
        ),
    )(taper_start, taper_stop, freq_index, traces, kernel)
    return pl.pallas_call(
        inverse,
        out_shape=jax.ShapeDtypeStruct((ROWS, RCV, TIME), jnp.float32),
        in_specs=[hbm] * 2,
        out_specs=hbm,
        scratch_shapes=[
            pltpu.VMEM((2, RCV, 2 * LANES), jnp.bfloat16),
            pltpu.VMEM((2 * BAND_FREQUENCIES, TIME), jnp.bfloat16),
            pltpu.VMEM((256, TIME), jnp.bfloat16),
            pltpu.VMEM((ROWS * RCV, 256), jnp.bfloat16),
            pltpu.VMEM((TIME // PIECE, ROWS, RCV, PIECE), jnp.float32),
            dma((2,)),
            dma((TIME // PIECE,)),
        ],
        compiler_params=pltpu.CompilerParams(vmem_limit_bytes=60 * 1024 * 1024),
        cost_estimate=pl.CostEstimate(
            flops=2 * 8_400_000, bytes_accessed=1024 * 1024, transcendentals=0
        ),
    )(response, table)


def solution(mesh):
    in_specs = (P(None, "rcv", "frq"), P("rcv"), P("rcv"), P(), P(None, "frq", "rcv", None))
    out_specs = P(None, "rcv", "frq")
    return jax.shard_map(
        per_device, mesh=mesh, in_specs=in_specs, out_specs=out_specs, check_vma=False
    )
```

```python
import math

import jax
import jax.numpy as jnp
from jax import lax
from jax.experimental import pallas as pl
from jax.experimental.pallas import tpu as pltpu
from jax.sharding import PartitionSpec as P

BAND_FREQUENCIES = 16
PADDED_LENGTH = 3072
MESH = pl.DeviceIdType.MESH

ROWS = 32
RCV = 16
TIME = 512
FREQS = 4
PLANE = 16
LINE = 8
RING = 16
GROUPS = 4
FC = 2 * FREQS
LANES = FC * ROWS
SRC = 128
HALF = ROWS // 2
PIECE = 256
PLANE_STEPS = (
    (2, 2), (2, 1), (2, 3), (1, 2), (3, 2), (1, 1), (1, 3), (3, 1),
    (3, 3), (2, 0), (0, 2), (1, 0), (3, 0), (0, 1), (0, 3),
)


def iota(shape, axis):
    return lax.broadcasted_iota(jnp.int32, shape, axis)


def column(ref, count, shape, first=0):
    rows = shape[0]
    each = rows // count
    row = iota(shape, 0) // each
    out = jnp.full(shape, ref[first], jnp.int32)
    for i in range(1, count):
        out = jnp.where(row == i, ref[first + i], out)
    return out


def tables(freq_ref, first_sample):
    shape = (2 * BAND_FREQUENCIES, TIME)
    bins = column(freq_ref, BAND_FREQUENCIES, shape)
    steps = bins * (first_sample + iota(shape, 1)) + (iota(shape, 0) % 2) * (PADDED_LENGTH // 4)
    steps = steps.astype(jnp.float32)
    steps = steps - jnp.floor(steps * (1.0 / PADDED_LENGTH)) * PADDED_LENGTH
    steps = jnp.where(steps < 0, steps + PADDED_LENGTH, steps)
    steps = jnp.where(steps >= PADDED_LENGTH, steps - PADDED_LENGTH, steps)
    x = (jnp.abs(steps - PADDED_LENGTH // 2) - PADDED_LENGTH // 4) * (2.0 * math.pi / PADDED_LENGTH)
    y = x * x
    poly = jnp.full(shape, -1.0 / math.factorial(11), jnp.float32)
    for power in (9, 7, 5, 3, 1):
        sign = 1.0 if power % 4 == 1 else -1.0
        poly = poly * y + sign / math.factorial(power)
    return x * poly


def body(
    index_hbm,
    traces_ref,
    kernel_ref,
    response_ref,
    table_ref,
    index_ref,
    tr_buf,
    kbuf,
    pown,
    pside,
    pbuf,
    fbuf,
    gbuf,
    part,
    pout,
    zbuf,
    local_sem,
    ks_sem,
    kr_sem,
    side_sem,
    fs_sem,
    gs_sem,
    gr_sem,
    zs_sem,
    zr_sem,
    rs_sem,
):
    rcv = lax.axis_index("rcv")
    frq = lax.axis_index("frq")
    plane = rcv // LINE
    line = rcv % LINE
    high = frq // 2
    core = frq % 2
    ring = high * LINE + line
    row = plane // 4
    col = plane % 4

    on_plane = []
    for across, down in PLANE_STEPS:
        peer = ((row + down) % 4) * 4 + (col + across) % 4
        on_plane.append((peer, (peer * LINE + line, high * 2 + 1)))
    on_ring = []
    for i in range(RING - 1):
        peer = i + (i + RING - ring) // RING
        on_ring.append((peer, (plane * LINE + peer % LINE, (peer // LINE) * 2 + 1)))
    opposite = (rcv, (1 - high) * 2 + 1)
    sibling = (rcv, high * 2 + 1 - core)

    barrier = pltpu.get_barrier_semaphore()

    def greet(device):
        pl.semaphore_signal(barrier, inc=1, device_id=device, device_id_type=MESH)

    @pl.when(core == 1)
    def _():
        for _, device in on_ring + on_plane:
            greet(device)
        greet(sibling)
        for peer, _ in on_plane:
            greet((peer * LINE + line, high * 2))

    @pl.when(core == 0)
    def _():
        greet(sibling)

    traces_copy = pltpu.make_async_copy(traces_ref, tr_buf, local_sem.at[0])
    traces_copy.start()
    index_copy = pltpu.make_async_copy(index_hbm, index_ref, local_sem.at[2])
    index_copy.start()
    index_copy.wait()
    table = tables(index_ref, frq * TIME).astype(jnp.bfloat16)
    table_ref[...] = table

    sample = frq * TIME + iota((RCV, TIME), 1)
    start = column(index_ref, RCV, (RCV, TIME), BAND_FREQUENCIES)
    stop = column(index_ref, RCV, (RCV, TIME), BAND_FREQUENCIES + RCV)
    window = jnp.where((sample >= start) & (sample < stop), 1.0, 0.0).astype(jnp.bfloat16)
    traces_copy.wait()
    tapered = (tr_buf[...] * window[None]).reshape(ROWS * RCV, TIME)
    sums = lax.dot_general(
        table, tapered, (((1,), (1,)), ((), ())), preferred_element_type=jnp.float32
    )
    for j in range(GROUPS):
        for half in range(2):
            piece = sums[j * FC : (j + 1) * FC, half * 256 : (half + 1) * 256]
            pown[j, half * FC : (half + 1) * FC] = piece

    def columns(peer):
        return kernel_ref.at[:, :, :, pl.ds(pl.multiple_of(peer * SRC, SRC), SRC)]

    def remote(source, target, send_sem, recv_sem, device):
        return pltpu.make_async_remote_copy(
            src_ref=source,
            dst_ref=target,
            send_sem=send_sem,
            recv_sem=recv_sem,
            device_id=device,
            device_id_type=MESH,
        )

    def kernel_copy(group, to, slot, device):
        return remote(
            columns(to), kbuf.at[group, :, :, slot], ks_sem.at[to], kr_sem.at[group, slot], device
        )

    side_copy = remote(pown, pside, side_sem.at[0], side_sem.at[1], sibling)
    response_copy = remote(response_ref, response_ref, rs_sem.at[0], rs_sem.at[1], sibling)

    @pl.when(core == 0)
    def _():
        pl.semaphore_wait(barrier, PLANE)
        side_copy.start()
        for peer, device in on_plane:
            kernel_copy(0, peer, plane, device).start()
        kernel_copy(0, plane, plane, sibling).start()
        side_copy.wait_send()
        for peer, device in on_plane:
            kernel_copy(0, peer, plane, device).wait_send()
        kernel_copy(0, plane, plane, sibling).wait_send()
        response_copy.wait_recv()

    @pl.when(core == 1)
    def _():
        own_copy = pltpu.make_async_copy(
            columns(plane), kbuf.at[1, :, :, plane], local_sem.at[1]
        )
        own_copy.start()

        side_copy.wait_recv()
        for j in range(GROUPS):
            pown[j] = pown[j] + pside[j]
        for c in range(2):
            pbuf[c] = pown[(1 - high) * 2 + c].astype(jnp.bfloat16)

        pl.semaphore_wait(barrier, PLANE + RING - 1)

        sums_copy = remote(pbuf, fbuf, fs_sem.at[0], fs_sem.at[1], opposite)
        sums_copy.start()
        for peer, device in on_plane:
            kernel_copy(1, peer, plane, device).start()

        spread = (FC, HALF, HALF * RCV)
        own_row = iota(spread, 2) // RCV == iota(spread, 1)
        pick = iota((RCV, HALF * RCV), 1) % RCV == iota((RCV, HALF * RCV), 0)
        pick = jnp.where(pick, 1.0, 0.0).astype(jnp.bfloat16)
        sums_copy.wait_recv()
        for c in range(2):
            total = pown[high * 2 + c] + fbuf[c].astype(jnp.float32)
            total = total * (1.0 / math.sqrt(PADDED_LENGTH))
            for half in range(2):
                wide = jnp.broadcast_to(total[half * FC : (half + 1) * FC][:, None, :], spread)
                wide = jnp.where(own_row, wide, 0.0).astype(jnp.bfloat16)
                spectra = lax.dot_general(
                    pick,
                    wide.reshape(FC * HALF, HALF * RCV),
                    (((1,), (1,)), ((), ())),
                    preferred_element_type=jnp.float32,
                )
                at = c * LANES + half * 128
                gbuf[plane, :, at : at + 128] = spectra.astype(jnp.bfloat16)

        def spectra_copy(to, slot, device):
            return remote(gbuf.at[plane], gbuf.at[slot], gs_sem.at[to], gr_sem.at[slot], device)

        for peer, device in on_plane:
            spectra_copy(peer, plane, device).start()

        own_copy.wait()
        kernel_copy(0, plane, plane, sibling).wait_recv()
        for peer, device in on_plane:
            kernel_copy(0, peer, peer, device).wait_recv()
            kernel_copy(1, peer, peer, device).wait_recv()
        for peer, device in on_plane:
            spectra_copy(peer, peer, device).wait_recv()

        for group in range(2):
            flipped = []
            for half in range(2):
                at = group * LANES + half * 128
                block = gbuf[:, :, at : at + 128].reshape(PLANE * RCV, 128)
                flipped.append(block.astype(jnp.float32).T)
            for pair in range(FREQS // 2):
                halves = []
                for f in (pair * 2, pair * 2 + 1):
                    at = f * 2 * HALF
                    real = [block[at : at + HALF] for block in flipped]
                    imag = [block[at + HALF : at + 2 * HALF] for block in flipped]
                    left = jnp.concatenate(real + imag, axis=0).astype(jnp.bfloat16)
                    right = jnp.concatenate(imag + [-block for block in real], axis=0)
                    right = right.astype(jnp.bfloat16)
                    halves.append(
                        jnp.dot(
                            left,
                            kbuf[group, 0, f].reshape(PLANE * RCV, SRC),
                            preferred_element_type=jnp.float32,
                        )
                        + jnp.dot(
                            right,
                            kbuf[group, 1, f].reshape(PLANE * RCV, SRC),
                            preferred_element_type=jnp.float32,
                        )
                    )
                turned = jnp.concatenate(halves, axis=0).T
                at = group * LANES + pair * 128
                part[:, at : at + 128] = turned
                pout[:, at : at + 128] = turned.astype(jnp.bfloat16)

        def source_rows(place):
            return pl.ds(pl.multiple_of((place % LINE) * RCV, RCV), RCV)

        def ring_copy(to, slot, device):
            return remote(
                pout.at[source_rows(to)], zbuf.at[slot], zs_sem.at[to], zr_sem.at[slot], device
            )

        for peer, device in on_ring:
            ring_copy(peer, ring, device).start()

        near = part[source_rows(ring)]
        far = jnp.zeros((RCV, 2 * LANES), jnp.float32)

        for peer, device in on_plane:
            kernel_copy(1, peer, plane, device).wait_send()
            spectra_copy(peer, plane, device).wait_send()
        sums_copy.wait_send()
        for step in range(1, LINE):
            peer = high * LINE + (line + step) % LINE
            ring_copy(peer, peer, opposite).wait_recv()
            near = near + zbuf[peer].astype(jnp.float32)
        for step in range(LINE):
            peer = (1 - high) * LINE + (line + LINE - 1 - step) % LINE
            ring_copy(peer, peer, opposite).wait_recv()
            far = far + zbuf[peer].astype(jnp.float32)
        response_ref[high] = near.astype(jnp.bfloat16)
        response_ref[1 - high] = far.astype(jnp.bfloat16)

        response_copy.start()
        for peer, device in on_ring:
            ring_copy(peer, ring, device).wait_send()
        response_copy.wait_send()


def inverse(response, table, out_hbm, texp, lhs, result, out_sem):
    own = iota((8, RCV, 128), 2) % 8 == iota((8, RCV, 128), 0)
    own = jnp.where(own, 1.0, 0.0).astype(jnp.bfloat16)
    slot = iota((RCV, 128), 1) // 8 % 4
    rows = table[...].astype(jnp.float32)
    for m in range(2):
        for q in range(4):
            block = []
            for i in range(4):
                row = (4 * m + i) * 4 + q
                block.append(jnp.broadcast_to(rows[row : row + 1], (8, TIME)))
            at = m * 128 + 32 * q
            texp[at : at + 32] = jnp.concatenate(block, axis=0).astype(jnp.bfloat16)
    for m in range(2):
        tiles = []
        for i in range(4):
            tiles.append(response[m, :, i * 128 : (i + 1) * 128].astype(jnp.float32))
        for a in range(ROWS // 8):
            merged = tiles[a]
            for i in range(4):
                if i != a:
                    turned = pltpu.roll(tiles[i], 8 * (i - a) % 128, 1)
                    merged = jnp.where(slot == i, turned, merged)
            terms = merged.astype(jnp.bfloat16)[None] * own
            lhs[a * 128 : (a + 1) * 128, m * 128 : (m + 1) * 128] = terms.reshape(128, 128)
    pieces = []
    for n in range(TIME // PIECE):
        samples = slice(n * PIECE, (n + 1) * PIECE)
        traces_out = jnp.dot(lhs[...], texp[:, samples], preferred_element_type=jnp.float32)
        traces_out = traces_out * (1.0 / math.sqrt(BAND_FREQUENCIES))
        result[n] = traces_out.reshape(ROWS, RCV, PIECE)
        pieces.append(
            pltpu.make_async_copy(result.at[n], out_hbm.at[:, :, samples], out_sem.at[n])
        )
        pieces[-1].start()
    for piece in pieces:
        piece.wait()


def per_device(traces, taper_start, taper_stop, freq_index, kernel):
    hbm = pl.BlockSpec(memory_space=pltpu.HBM)
    vmem = pl.BlockSpec(memory_space=pltpu.VMEM)
    dma = pltpu.SemaphoreType.DMA
    response, table = pl.pallas_call(
        body,
        out_shape=[
            jax.ShapeDtypeStruct((2, RCV, 2 * LANES), jnp.bfloat16),
            jax.ShapeDtypeStruct((2 * BAND_FREQUENCIES, TIME), jnp.bfloat16),
        ],
        in_specs=[hbm] * 3,
        out_specs=[vmem] * 2,
        scratch_shapes=[
            pltpu.SMEM((BAND_FREQUENCIES + 2 * RCV,), jnp.int32),
            pltpu.VMEM((ROWS, RCV, TIME), jnp.bfloat16),
            pltpu.VMEM((2, 2, FREQS, PLANE, RCV, SRC), jnp.bfloat16),
            pltpu.VMEM((GROUPS, 2 * FC, HALF * RCV), jnp.float32),
            pltpu.VMEM((GROUPS, 2 * FC, HALF * RCV), jnp.float32),
            pltpu.VMEM((2, 2 * FC, HALF * RCV), jnp.bfloat16),
            pltpu.VMEM((2, 2 * FC, HALF * RCV), jnp.bfloat16),
            pltpu.VMEM((PLANE, RCV, 2 * LANES), jnp.bfloat16),
            pltpu.VMEM((SRC, 2 * LANES), jnp.float32),
            pltpu.VMEM((SRC, 2 * LANES), jnp.bfloat16),
            pltpu.VMEM((RING, RCV, 2 * LANES), jnp.bfloat16),
            dma((3,)),
            dma((PLANE,)),
            dma((2, PLANE)),
            dma((2,)),
            dma((2,)),
            dma((PLANE,)),
            dma((PLANE,)),
            dma((RING,)),
            dma((RING,)),
            dma((2,)),
        ],
        compiler_params=pltpu.CompilerParams(
            collective_id=0, has_side_effects=True, vmem_limit_bytes=54784 * 1024
        ),
        cost_estimate=pl.CostEstimate(
            flops=2 * 40_000_000, bytes_accessed=1024 * 1024, transcendentals=0
        ),
    )(jnp.concatenate([freq_index, taper_start, taper_stop]), traces, kernel)
    return pl.pallas_call(
        inverse,
        out_shape=jax.ShapeDtypeStruct((ROWS, RCV, TIME), jnp.float32),
        in_specs=[vmem] * 2,
        out_specs=hbm,
        scratch_shapes=[
            pltpu.VMEM((256, TIME), jnp.bfloat16),
            pltpu.VMEM((ROWS * RCV, 256), jnp.bfloat16),
            pltpu.VMEM((TIME // PIECE, ROWS, RCV, PIECE), jnp.float32),
            dma((TIME // PIECE,)),
        ],
        compiler_params=pltpu.CompilerParams(vmem_limit_bytes=16 * 1024 * 1024),
        cost_estimate=pl.CostEstimate(
            flops=2 * 8_400_000, bytes_accessed=1024 * 1024, transcendentals=0
        ),
    )(response, table)


def solution(mesh):
    in_specs = (P(None, "rcv", "frq"), P("rcv"), P("rcv"), P(), P(None, "frq", "rcv", None))
    out_specs = P(None, "rcv", "frq")
    return jax.shard_map(
        per_device, mesh=mesh, in_specs=in_specs, out_specs=out_specs, check_vma=False
    )
```

```python
import math

import jax
import jax.numpy as jnp
from jax import lax
from jax.experimental import pallas as pl
from jax.experimental.pallas import tpu as pltpu
from jax.sharding import PartitionSpec as P

BAND_FREQUENCIES = 16
PADDED_LENGTH = 3072
MESH = pl.DeviceIdType.MESH

ROWS = 32
RCV = 16
TIME = 512
FREQS = 4
PLANE = 16
LINE = 8
RING = 16
GROUPS = 4
FC = 2 * FREQS
LANES = FC * ROWS
SRC = 128
HALF = ROWS // 2
PIECE = 256
PLANE_STEPS = (
    (2, 2), (2, 1), (2, 3), (1, 2), (3, 2), (1, 1), (1, 3), (3, 1),
    (3, 3), (2, 0), (0, 2), (1, 0), (3, 0), (0, 1), (0, 3),
)


def iota(shape, axis):
    return lax.broadcasted_iota(jnp.int32, shape, axis)


def column(ref, count, shape, first=0):
    rows = shape[0]
    each = rows // count
    row = iota(shape, 0) // each
    out = jnp.full(shape, ref[first], jnp.int32)
    for i in range(1, count):
        out = jnp.where(row == i, ref[first + i], out)
    return out


def tables(freq_ref, first_sample):
    shape = (2 * BAND_FREQUENCIES, TIME)
    bins = column(freq_ref, BAND_FREQUENCIES, shape)
    steps = bins * (first_sample + iota(shape, 1)) + (iota(shape, 0) % 2) * (PADDED_LENGTH // 4)
    steps = steps.astype(jnp.float32)
    steps = steps - jnp.floor(steps * (1.0 / PADDED_LENGTH)) * PADDED_LENGTH
    steps = jnp.where(steps < 0, steps + PADDED_LENGTH, steps)
    steps = jnp.where(steps >= PADDED_LENGTH, steps - PADDED_LENGTH, steps)
    x = (jnp.abs(steps - PADDED_LENGTH // 2) - PADDED_LENGTH // 4) * (2.0 * math.pi / PADDED_LENGTH)
    y = x * x
    poly = jnp.full(shape, -1.0 / math.factorial(11), jnp.float32)
    for power in (9, 7, 5, 3, 1):
        sign = 1.0 if power % 4 == 1 else -1.0
        poly = poly * y + sign / math.factorial(power)
    return x * poly


def body(
    index_hbm,
    traces_ref,
    kernel_ref,
    response_ref,
    table_ref,
    index_ref,
    tr_buf,
    kbuf,
    pown,
    pside,
    pbuf,
    fbuf,
    gbuf,
    part,
    pout,
    zbuf,
    local_sem,
    ks_sem,
    kr_sem,
    side_sem,
    fs_sem,
    gs_sem,
    gr_sem,
    zs_sem,
    zr_sem,
    rs_sem,
):
    rcv = lax.axis_index("rcv")
    frq = lax.axis_index("frq")
    plane = rcv // LINE
    line = rcv % LINE
    high = frq // 2
    core = frq % 2
    ring = high * LINE + line
    row = plane // 4
    col = plane % 4

    on_plane = []
    for across, down in PLANE_STEPS:
        peer = ((row + down) % 4) * 4 + (col + across) % 4
        on_plane.append((peer, (peer * LINE + line, high * 2 + 1)))
    on_ring = []
    for i in range(RING - 1):
        peer = i + (i + RING - ring) // RING
        on_ring.append((peer, (plane * LINE + peer % LINE, (peer // LINE) * 2 + 1)))
    opposite = (rcv, (1 - high) * 2 + 1)
    sibling = (rcv, high * 2 + 1 - core)

    barrier = pltpu.get_barrier_semaphore()

    def greet(device):
        pl.semaphore_signal(barrier, inc=1, device_id=device, device_id_type=MESH)

    @pl.when(core == 1)
    def _():
        for _, device in on_ring + on_plane:
            greet(device)
        greet(sibling)
        for peer, _ in on_plane:
            greet((peer * LINE + line, high * 2))

    @pl.when(core == 0)
    def _():
        greet(sibling)

    traces_copy = pltpu.make_async_copy(traces_ref, tr_buf, local_sem.at[0])
    traces_copy.start()
    index_copy = pltpu.make_async_copy(index_hbm, index_ref, local_sem.at[2])
    index_copy.start()
    index_copy.wait()
    table = tables(index_ref, frq * TIME).astype(jnp.bfloat16)
    table_ref[...] = table

    sample = frq * TIME + iota((RCV, TIME), 1)
    start = column(index_ref, RCV, (RCV, TIME), BAND_FREQUENCIES)
    stop = column(index_ref, RCV, (RCV, TIME), BAND_FREQUENCIES + RCV)
    window = jnp.where((sample >= start) & (sample < stop), 1.0, 0.0).astype(jnp.bfloat16)
    traces_copy.wait()
    tapered = (tr_buf[...] * window[None]).reshape(ROWS * RCV, TIME)
    sums = lax.dot_general(
        table, tapered, (((1,), (1,)), ((), ())), preferred_element_type=jnp.float32
    )
    for j in range(GROUPS):
        for half in range(2):
            piece = sums[j * FC : (j + 1) * FC, half * 256 : (half + 1) * 256]
            pown[j, half * FC : (half + 1) * FC] = piece

    def columns(peer):
        return kernel_ref.at[:, :, :, pl.ds(pl.multiple_of(peer * SRC, SRC), SRC)]

    def remote(source, target, send_sem, recv_sem, device):
        return pltpu.make_async_remote_copy(
            src_ref=source,
            dst_ref=target,
            send_sem=send_sem,
            recv_sem=recv_sem,
            device_id=device,
            device_id_type=MESH,
        )

    def kernel_copy(group, to, slot, device):
        return remote(
            columns(to), kbuf.at[group, :, :, slot], ks_sem.at[to], kr_sem.at[group, slot], device
        )

    side_copy = remote(pown, pside, side_sem.at[0], side_sem.at[1], sibling)
    response_copy = remote(response_ref, response_ref, rs_sem.at[0], rs_sem.at[1], sibling)

    @pl.when(core == 0)
    def _():
        pl.semaphore_wait(barrier, PLANE)
        side_copy.start()
        for peer, device in on_plane:
            kernel_copy(0, peer, plane, device).start()
        kernel_copy(0, plane, plane, sibling).start()
        side_copy.wait_send()
        for peer, device in on_plane:
            kernel_copy(0, peer, plane, device).wait_send()
        kernel_copy(0, plane, plane, sibling).wait_send()
        response_copy.wait_recv()

    @pl.when(core == 1)
    def _():
        own_copy = pltpu.make_async_copy(
            columns(plane), kbuf.at[1, :, :, plane], local_sem.at[1]
        )
        own_copy.start()

        side_copy.wait_recv()
        for j in range(GROUPS):
            pown[j] = pown[j] + pside[j]
        for c in range(2):
            pbuf[c] = pown[(1 - high) * 2 + c].astype(jnp.bfloat16)

        pl.semaphore_wait(barrier, PLANE + RING - 1)

        sums_copy = remote(pbuf, fbuf, fs_sem.at[0], fs_sem.at[1], opposite)
        sums_copy.start()
        for peer, device in on_plane:
            kernel_copy(1, peer, plane, device).start()

        spread = (FC, HALF, HALF * RCV)
        own_row = iota(spread, 2) // RCV == iota(spread, 1)
        pick = iota((RCV, HALF * RCV), 1) % RCV == iota((RCV, HALF * RCV), 0)
        pick = jnp.where(pick, 1.0, 0.0).astype(jnp.bfloat16)
        sums_copy.wait_recv()
        for c in range(2):
            total = pown[high * 2 + c] + fbuf[c].astype(jnp.float32)
            total = total * (1.0 / math.sqrt(PADDED_LENGTH))
            for half in range(2):
                wide = jnp.broadcast_to(total[half * FC : (half + 1) * FC][:, None, :], spread)
                wide = jnp.where(own_row, wide, 0.0).astype(jnp.bfloat16)
                spectra = lax.dot_general(
                    pick,
                    wide.reshape(FC * HALF, HALF * RCV),
                    (((1,), (1,)), ((), ())),
                    preferred_element_type=jnp.float32,
                )
                at = c * LANES + half * 128
                gbuf[plane, :, at : at + 128] = spectra.astype(jnp.bfloat16)

        def spectra_copy(to, slot, device):
            return remote(gbuf.at[plane], gbuf.at[slot], gs_sem.at[to], gr_sem.at[slot], device)

        for i in range(PLANE - 1):
            peer = i + (i + PLANE - plane) // PLANE
            spectra_copy(peer, plane, (peer * LINE + line, high * 2 + 1)).start()

        own_copy.wait()
        kernel_copy(0, plane, plane, sibling).wait_recv()
        for peer, device in on_plane:
            kernel_copy(0, peer, peer, device).wait_recv()
            kernel_copy(1, peer, peer, device).wait_recv()
        for peer, device in on_plane:
            spectra_copy(peer, peer, device).wait_recv()

        for group in range(2):
            flipped = []
            for half in range(2):
                at = group * LANES + half * 128
                block = gbuf[:, :, at : at + 128].reshape(PLANE * RCV, 128)
                flipped.append(block.astype(jnp.float32).T)
            for pair in range(FREQS // 2):
                halves = []
                for f in (pair * 2, pair * 2 + 1):
                    at = f * 2 * HALF
                    real = [block[at : at + HALF] for block in flipped]
                    imag = [block[at + HALF : at + 2 * HALF] for block in flipped]
                    left = jnp.concatenate(real + imag, axis=0).astype(jnp.bfloat16)
                    right = jnp.concatenate(imag + [-block for block in real], axis=0)
                    right = right.astype(jnp.bfloat16)
                    halves.append(
                        jnp.dot(
                            left,
                            kbuf[group, 0, f].reshape(PLANE * RCV, SRC),
                            preferred_element_type=jnp.float32,
                        )
                        + jnp.dot(
                            right,
                            kbuf[group, 1, f].reshape(PLANE * RCV, SRC),
                            preferred_element_type=jnp.float32,
                        )
                    )
                turned = jnp.concatenate(halves, axis=0).T
                at = group * LANES + pair * 128
                part[:, at : at + 128] = turned
                pout[:, at : at + 128] = turned.astype(jnp.bfloat16)

        def source_rows(place):
            return pl.ds(pl.multiple_of((place % LINE) * RCV, RCV), RCV)

        def ring_copy(to, slot, device):
            return remote(
                pout.at[source_rows(to)], zbuf.at[slot], zs_sem.at[to], zr_sem.at[slot], device
            )

        for peer, device in on_ring:
            ring_copy(peer, ring, device).start()

        near = part[source_rows(ring)]
        far = jnp.zeros((RCV, 2 * LANES), jnp.float32)

        for peer, device in on_plane:
            kernel_copy(1, peer, plane, device).wait_send()
            spectra_copy(peer, plane, device).wait_send()
        sums_copy.wait_send()
        for peer, device in on_ring:
            ring_copy(peer, ring, device).wait_send()
        for step in range(1, LINE):
            peer = high * LINE + (line + step) % LINE
            ring_copy(peer, peer, opposite).wait_recv()
            near = near + zbuf[peer].astype(jnp.float32)
        for step in range(LINE):
            peer = (1 - high) * LINE + (line + LINE - 1 - step) % LINE
            ring_copy(peer, peer, opposite).wait_recv()
            far = far + zbuf[peer].astype(jnp.float32)
        response_ref[high] = near.astype(jnp.bfloat16)
        response_ref[1 - high] = far.astype(jnp.bfloat16)

        response_copy.start()
        response_copy.wait_send()


def inverse(response, table, out_hbm, texp, lhs, result, out_sem):
    own = iota((8, RCV, 128), 2) % 8 == iota((8, RCV, 128), 0)
    own = jnp.where(own, 1.0, 0.0).astype(jnp.bfloat16)
    slot = iota((RCV, 128), 1) // 8 % 4
    rows = table[...].astype(jnp.float32)
    for m in range(2):
        for q in range(4):
            block = []
            for i in range(4):
                row = (4 * m + i) * 4 + q
                block.append(jnp.broadcast_to(rows[row : row + 1], (8, TIME)))
            at = m * 128 + 32 * q
            texp[at : at + 32] = jnp.concatenate(block, axis=0).astype(jnp.bfloat16)
    for m in range(2):
        tiles = []
        for i in range(4):
            tiles.append(response[m, :, i * 128 : (i + 1) * 128].astype(jnp.float32))
        for a in range(ROWS // 8):
            merged = tiles[a]
            for i in range(4):
                if i != a:
                    turned = pltpu.roll(tiles[i], 8 * (i - a) % 128, 1)
                    merged = jnp.where(slot == i, turned, merged)
            terms = merged.astype(jnp.bfloat16)[None] * own
            lhs[a * 128 : (a + 1) * 128, m * 128 : (m + 1) * 128] = terms.reshape(128, 128)
    pieces = []
    for n in range(TIME // PIECE):
        samples = slice(n * PIECE, (n + 1) * PIECE)
        traces_out = jnp.dot(lhs[...], texp[:, samples], preferred_element_type=jnp.float32)
        traces_out = traces_out * (1.0 / math.sqrt(BAND_FREQUENCIES))
        result[n] = traces_out.reshape(ROWS, RCV, PIECE)
        pieces.append(
            pltpu.make_async_copy(result.at[n], out_hbm.at[:, :, samples], out_sem.at[n])
        )
        pieces[-1].start()
    for piece in pieces:
        piece.wait()


def per_device(traces, taper_start, taper_stop, freq_index, kernel):
    hbm = pl.BlockSpec(memory_space=pltpu.HBM)
    vmem = pl.BlockSpec(memory_space=pltpu.VMEM)
    dma = pltpu.SemaphoreType.DMA
    response, table = pl.pallas_call(
        body,
        out_shape=[
            jax.ShapeDtypeStruct((2, RCV, 2 * LANES), jnp.bfloat16),
            jax.ShapeDtypeStruct((2 * BAND_FREQUENCIES, TIME), jnp.bfloat16),
        ],
        in_specs=[hbm] * 3,
        out_specs=[vmem] * 2,
        scratch_shapes=[
            pltpu.SMEM((BAND_FREQUENCIES + 2 * RCV,), jnp.int32),
            pltpu.VMEM((ROWS, RCV, TIME), jnp.bfloat16),
            pltpu.VMEM((2, 2, FREQS, PLANE, RCV, SRC), jnp.bfloat16),
            pltpu.VMEM((GROUPS, 2 * FC, HALF * RCV), jnp.float32),
            pltpu.VMEM((GROUPS, 2 * FC, HALF * RCV), jnp.float32),
            pltpu.VMEM((2, 2 * FC, HALF * RCV), jnp.bfloat16),
            pltpu.VMEM((2, 2 * FC, HALF * RCV), jnp.bfloat16),
            pltpu.VMEM((PLANE, RCV, 2 * LANES), jnp.bfloat16),
            pltpu.VMEM((SRC, 2 * LANES), jnp.float32),
            pltpu.VMEM((SRC, 2 * LANES), jnp.bfloat16),
            pltpu.VMEM((RING, RCV, 2 * LANES), jnp.bfloat16),
            dma((3,)),
            dma((PLANE,)),
            dma((2, PLANE)),
            dma((2,)),
            dma((2,)),
            dma((PLANE,)),
            dma((PLANE,)),
            dma((RING,)),
            dma((RING,)),
            dma((2,)),
        ],
        compiler_params=pltpu.CompilerParams(
            collective_id=0, has_side_effects=True, vmem_limit_bytes=54784 * 1024
        ),
        cost_estimate=pl.CostEstimate(
            flops=2 * 40_000_000, bytes_accessed=1024 * 1024, transcendentals=0
        ),
    )(jnp.concatenate([freq_index, taper_start, taper_stop]), traces, kernel)
    return pl.pallas_call(
        inverse,
        out_shape=jax.ShapeDtypeStruct((ROWS, RCV, TIME), jnp.float32),
        in_specs=[vmem] * 2,
        out_specs=hbm,
        scratch_shapes=[
            pltpu.VMEM((256, TIME), jnp.bfloat16),
            pltpu.VMEM((ROWS * RCV, 256), jnp.bfloat16),
            pltpu.VMEM((TIME // PIECE, ROWS, RCV, PIECE), jnp.float32),
            dma((TIME // PIECE,)),
        ],
        compiler_params=pltpu.CompilerParams(vmem_limit_bytes=16 * 1024 * 1024),
        cost_estimate=pl.CostEstimate(
            flops=2 * 8_400_000, bytes_accessed=1024 * 1024, transcendentals=0
        ),
    )(response, table)


def solution(mesh):
    in_specs = (P(None, "rcv", "frq"), P("rcv"), P("rcv"), P(), P(None, "frq", "rcv", None))
    out_specs = P(None, "rcv", "frq")
    return jax.shard_map(
        per_device, mesh=mesh, in_specs=in_specs, out_specs=out_specs, check_vma=False
    )
```
